32 devices in a mesh: dp: 8 (over z, y), seq: 4 (over x, core).
Axes of the slice: x: 2, y: 2, z: 4, core: 2. Of those that a mesh axis runs over, the one named last changes fastest.
Arguments:
- inputs: bfloat16 [8, 512, 4096], P('dp', 'seq'), may hold values from -6 to 6
- raw_step: bfloat16 [8, 512, 64], P('dp', 'seq'), may hold values from -5 to 5
- write_keys: bfloat16 [8, 512, 128], P('dp', 'seq'), may hold values from -0.5 to 0.5
- read_keys: bfloat16 [8, 512, 128], P('dp', 'seq'), may hold values from -0.5 to 0.5
- grad_out: bfloat16 [8, 512, 4096], P('dp', 'seq'), may hold values from -6 to 6
- decay_log: float32 [64], P('seq'), as said below
- skip_gain: float32 [64], P('seq'), may hold values from 0.5 to 1.5
- step_bias: float32 [64], P('seq'), may hold values from -1 to 1
Outputs:
- grad_x: bfloat16 [8, 512, 4096], P('dp', 'seq')
- grad_step: bfloat16 [8, 512, 64], P('dp', 'seq')
- grad_write: bfloat16 [8, 512, 128], P('dp', 'seq')
- grad_read: bfloat16 [8, 512, 128], P('dp', 'seq')
- grad_params: float32 [3, 64], P(None, 'seq')
The draws below stay inside these ranges and needn't reach their ends.
Inputs may be any that keep to these rules, and one draw needn't show every extreme that they name: exp(decay_log) lies between 0.2 / 512 and 1 / 20.
All inputs are finite; a program needn't handle non-finite values.
Results may differ from the reference program's by a relative error of at most 0.002.
Values may be sent and summed in bfloat16 or wider, within the bound.
A program may use at most 128 MiB of HBM per device.

```python
import jax
import jax.numpy as jnp
from jax import lax

HEADS = 64
HDIM = 64
NSTATE = 128
SPAN = 256
SEQ = 512
REPL = 8
HEAD_DEV = 16
N_SEQ = 4


def draw_decay_log(key, part):
    key = jax.random.fold_in(key, 11)
    pick_key, fast_key, slow_key = jax.random.split(key, 3)
    slow_share = 0.5
    slow_heads = jax.random.uniform(pick_key, (HEADS,), jnp.float32) < slow_share
    fast_rate = jnp.exp(jax.random.uniform(fast_key, (HEADS,), jnp.float32, jnp.log(1.0 / 40.0), jnp.log(1.0 / 20.0)))
    slow_rate = jnp.exp(jax.random.uniform(slow_key, (HEADS,), jnp.float32, jnp.log(0.2 / SEQ), jnp.log(1.5 / SEQ)))
    return jnp.log(jnp.where(slow_heads, slow_rate, fast_rate)).astype(jnp.float32)


def levels(key, dims, cuts, low, high):
    loudness = 1.0
    for position, parts in cuts:
        steps = jax.random.uniform(jax.random.fold_in(jax.random.fold_in(key, 6), position), (parts,), jnp.float32, low / len(cuts), high / len(cuts))
        loudness = loudness * jnp.repeat(jnp.exp(steps), dims[position] // parts).reshape((-1,) + (1,) * (len(dims) - 1 - position))
    return loudness


def centred(own_key, dims, width, bound, shards=(), kind=jnp.bfloat16):
    result = width * jax.random.normal(own_key, dims, jnp.float32)
    if shards:
        result = result * levels(own_key, dims, shards, -0.22, 0.18)
    return jnp.clip(result, -bound, bound).astype(kind)


def setup_inputs(seed: int = 0) -> dict:
    key_of = jax.random.split(jax.random.key(seed), 9)
    return {
        "inputs": centred(key_of[0], (REPL, SEQ, HEADS * HDIM), 1.0, 6.0, ((0, 8), (1, 4))),
        "raw_step": centred(key_of[1], (REPL, SEQ, HEADS), 1.0, 5.0, ((0, 8), (1, 4))),
        "write_keys": centred(key_of[2], (REPL, SEQ, NSTATE), NSTATE ** -0.5, 0.5, ((0, 8), (1, 4))),
        "read_keys": centred(key_of[3], (REPL, SEQ, NSTATE), NSTATE ** -0.5, 0.5, ((0, 8), (1, 4))),
        "grad_out": centred(key_of[4], (REPL, SEQ, HEADS * HDIM), 1.0, 6.0, ((0, 8), (1, 4))),
        "decay_log": draw_decay_log(jax.random.fold_in(key_of[8], 71), 0),
        "skip_gain": jnp.clip(0.5 + 1.0 * jax.random.uniform(key_of[6], (HEADS,), jnp.float32) ** levels(key_of[6], (HEADS,), ((0, 4),), -0.2, 0.2), 0.5, 1.5),
        "step_bias": jnp.clip(jax.random.uniform(key_of[7], (HEADS,), jnp.float32, -1.0, 1.0) * levels(key_of[7], (HEADS,), ((0, 4),), -0.4, 0.0), -1.0, 1.0),
    }


highest = lax.Precision.HIGHEST

def span_inner(pieces):
    block_scaled, block_decay, block_write, block_read = pieces
    scores = jnp.dot(block_read, block_write.T, precision=highest, preferred_element_type=jnp.float32)
    extent = block_decay.shape[0]
    causal = lax.broadcasted_iota(jnp.int32, (extent, extent), 0) >= lax.broadcasted_iota(jnp.int32, (extent, extent), 1)
    by_head = block_decay.T
    spread = by_head[:, :, None] - by_head[:, None, :]
    weights = jnp.exp(jnp.where(causal[None], spread, -jnp.inf)) * scores[None]
    within = jnp.einsum('hqs,shp->qhp', weights, block_scaled, precision=highest)
    to_end = jnp.exp(block_decay[-1:] - block_decay)
    end_state = jnp.einsum('sn,shp->hnp', block_write, block_scaled * to_end[:, :, None], precision=highest)
    return (within, end_state)

def entering_sequential(end_states, totals):

    def advance(running, pieces):
        span_state, span_total = pieces
        return (jnp.exp(span_total)[:, None, None] * running + span_state, running)
    initial = jnp.zeros(end_states.shape[1:], end_states.dtype)
    _, entering = lax.scan(advance, initial, (end_states, totals))
    return entering

def mixer_forward(inputs, raw_step, write_keys, read_keys, decay_log, skip_gain, step_bias):
    length, head_count, head_width = inputs.shape
    blocks = length // SPAN
    step_size = jax.nn.softplus(raw_step + step_bias[None, :])
    log_decay = -jnp.exp(decay_log)[None, :] * step_size
    scaled = (inputs * step_size[:, :, None]).reshape(blocks, SPAN, head_count, head_width)
    cumulative = jnp.cumsum(log_decay.reshape(blocks, SPAN, head_count), axis=1)
    write_blocks = write_keys.reshape(blocks, SPAN, -1)
    read_blocks = read_keys.reshape(blocks, SPAN, -1)
    within, end_states = lax.map(jax.checkpoint(span_inner), (scaled, cumulative, write_blocks, read_blocks))
    entering = entering_sequential(end_states, cumulative[:, -1, :])
    carried = jnp.einsum('kqn,khnp->kqhp', read_blocks, entering, precision=highest) * jnp.exp(cumulative)[:, :, :, None]
    return (within + carried).reshape(length, head_count, head_width) + skip_gain[None, :, None] * inputs

def replica_grads(pieces, decay_log, skip_gain, step_bias):
    inputs, raw_step, write_keys, read_keys, grad_out = pieces
    write_full = write_keys.astype(jnp.float32)
    read_full = read_keys.astype(jnp.float32)
    group_inputs = inputs.reshape(SEQ, N_SEQ, HEAD_DEV * HDIM).transpose(1, 0, 2)
    group_grad = grad_out.reshape(SEQ, N_SEQ, HEAD_DEV * HDIM).transpose(1, 0, 2)
    group_step = raw_step.reshape(SEQ, N_SEQ, HEAD_DEV).transpose(1, 0, 2)

    def one_group(group):
        part_inputs, part_grad, part_step, part_decay, part_skip, part_bias = group
        _, pullback = jax.vjp(mixer_forward, part_inputs.astype(jnp.float32).reshape(SEQ, HEAD_DEV, HDIM), part_step.astype(jnp.float32), write_full, read_full, part_decay, part_skip, part_bias)
        grads = pullback(part_grad.astype(jnp.float32).reshape(SEQ, HEAD_DEV, HDIM))
        return grads
    outs = lax.map(one_group, (group_inputs, group_grad, group_step, decay_log.reshape(N_SEQ, HEAD_DEV), skip_gain.reshape(N_SEQ, HEAD_DEV), step_bias.reshape(N_SEQ, HEAD_DEV)))
    grad_inputs = outs[0].transpose(1, 0, 2, 3).reshape(SEQ, HEADS * HDIM)
    grad_raw = outs[1].transpose(1, 0, 2).reshape(SEQ, HEADS)
    grad_write = lax.optimization_barrier(jnp.sum(outs[2], axis=0))
    grad_read = lax.optimization_barrier(jnp.sum(outs[3], axis=0))
    return (grad_inputs, grad_raw, grad_write, grad_read, outs[4].reshape(HEADS), outs[5].reshape(HEADS), outs[6].reshape(HEADS))

def reference(inputs, raw_step, write_keys, read_keys, grad_out, decay_log, skip_gain, step_bias):

    def replica(pieces):
        grads = replica_grads(pieces, decay_log, skip_gain, step_bias)
        return (grads[0].astype(jnp.bfloat16), grads[1].astype(jnp.bfloat16), grads[2].astype(jnp.bfloat16), grads[3].astype(jnp.bfloat16), jnp.stack([grads[4], grads[5], grads[6]]))
    grad_x, grad_step, grad_write, grad_read, per_replica = lax.map(replica, (inputs, raw_step, write_keys, read_keys, grad_out))
    grad_params = lax.optimization_barrier(jnp.sum(per_replica, axis=0)) / REPL
    return (grad_x, grad_step, grad_write, grad_read, grad_params)
```

```python
import functools

import jax
import jax.numpy as jnp
from jax import lax
from jax.experimental import pallas as pl
from jax.experimental.pallas import tpu as pltpu
from jax.sharding import PartitionSpec as P

LANES = 128
ROWS = 16
LOG2E = 1.4426950408889634
bf16 = jnp.bfloat16
f32 = jnp.float32


def iota(shape, dim):
    return lax.broadcasted_iota(jnp.int32, shape, dim)


def dot_nt(a, b):
    return lax.dot_general(a, b, (((1,), (1,)), ((), ())), preferred_element_type=f32)


def dot_nn(a, b):
    return jnp.dot(a, b, preferred_element_type=f32)


def split_two(v):
    hi = v.astype(bf16)
    return hi, (v - hi.astype(f32)).astype(bf16)


def scan_lanes(v, reverse):
    rows, length = v.shape
    width = min(256, length)
    r, c = iota((width, width), 0), iota((width, width), 1)
    keep = (r >= c) if reverse else (r <= c)
    ones = jnp.where(keep, 1.0, 0.0).astype(bf16)
    one = v.astype(bf16)
    rest = v - one.astype(f32)
    two = rest.astype(bf16)
    three = (rest - two.astype(f32)).astype(bf16)
    stacked = jnp.concatenate([one, two, three], axis=0)
    spots = list(range(0, length, width))
    carry = jnp.zeros((rows, 1), f32)
    out = {}
    for start in reversed(spots) if reverse else spots:
        part = dot_nn(stacked[:, start : start + width], ones)
        part = part[:rows] + (part[rows : 2 * rows] + part[2 * rows :]) + carry
        out[start] = part
        carry = part[:, :1] if reverse else part[:, width - 1 :]
    return jnp.concatenate([out[s] for s in spots], axis=1)


def prepare(raw, decay, bias, wide, small, arow, acol, dts, sig, rate, heads):
    length = raw.shape[0]
    wide[...] = jnp.zeros_like(wide)
    wide[:, :heads] = raw[...].astype(f32) + bias[...]
    z = wide[...].T[:heads]
    small[...] = jnp.zeros_like(small)
    small[0:1, :heads] = jnp.exp(decay[...])
    rate_col = jnp.broadcast_to(small[0:1, :], (LANES, LANES)).T[:heads]
    rate[...] = rate_col
    dt = jnp.maximum(z, 0.0) + jnp.log1p(jnp.exp(-jnp.abs(z)))
    dts[...] = dt
    sig[...] = 1.0 / (1.0 + jnp.exp(-z))
    a = scan_lanes(dt * (rate_col[:, :1] * -LOG2E), False)
    for h in range(heads):
        arow[h] = jnp.broadcast_to(a[h : h + 1, :], (8, length))
    below = a - jnp.log(dt) * LOG2E
    column = jnp.concatenate([below, jnp.zeros((LANES - heads, length), f32)], axis=0).T
    for h in range(heads):
        acol[h] = jnp.broadcast_to(column[:, h : h + 1], (length, LANES))


def tile(pair, s0, t0, width, diagonal, x, g, scr):
    w, m, vacc = scr["w"], scr["m"], scr["vacc"]
    lanes = pl.ds(pl.multiple_of(pair * LANES, LANES), LANES)
    srows, trows = pl.ds(s0, LANES), pl.ds(t0, width)
    xs = x[srows, lanes]
    gs = g[trows, lanes]
    low = iota((width, LANES), 1) < LANES // 2
    zero = jnp.zeros_like(gs)
    parts = (jnp.where(low, gs, zero), jnp.where(low, zero, gs))
    for k in range(2):
        w[k, :, :width] = dot_nt(xs, parts[k])
    lane = iota((ROWS, LANES), 1)
    at = [scr["arow"][2 * pair + k, :, trows] for k in range(2)]
    at = [jnp.concatenate([v] * (ROWS // 8), axis=0) for v in at]
    sums = [None, None]
    for c in range(LANES // ROWS):
        rows = pl.ds(s0 + c * ROWS, ROWS)
        here = slice(c * ROWS, (c + 1) * ROWS)
        s_tile = scr["score"][rows, trows]
        q = scr["q"][rows, trows]
        col = scr["col"][rows, :]
        for k in range(2):
            ac = scr["acol"][2 * pair + k, rows, :]
            gap = at[k] - jnp.concatenate([ac] * (width // LANES), axis=1)
            if diagonal:
                keep = iota((ROWS, width), 1) >= iota((ROWS, width), 0) + c * ROWS
                gap = jnp.where(keep, gap, -jnp.inf)
            lp = jnp.exp2(gap)
            wk = w[k, here, :width]
            q = q + lp * wk
            mk = lp * s_tile
            hi, lo = split_two(mk)
            m[2 * k, here, :width] = hi
            m[2 * k + 1, here, :width] = lo
            zk = mk * wk
            part = zk[:8] + zk[8:]
            sums[k] = part if sums[k] is None else sums[k] + part
            across = zk[:, :LANES]
            for j in range(1, width // LANES):
                across = across + zk[:, j * LANES : (j + 1) * LANES]
            total = jnp.sum(across, axis=1, keepdims=True)
            col = col + jnp.where(lane == 2 * pair + k, total, 0.0)
        scr["q"][rows, trows] = q
        scr["col"][rows, :] = col
    for k in range(2):
        scr["racc"][k, :, trows] += sums[k]
    v = None
    for k in range(2):
        for j in range(2):
            term = dot_nn(m[2 * k + j, :, :width], parts[k])
            v = term if v is None else v + term
    return v


def one_pair(pair, x, g, skip, dx, scr, length):
    lanes = pl.ds(pl.multiple_of(pair * LANES, LANES), LANES)
    scr["racc"][...] = jnp.zeros_like(scr["racc"])
    low = iota((1, LANES), 1) < LANES // 2
    gain = jnp.where(low, skip[2 * pair], skip[2 * pair + 1])
    blocks = length // LANES

    def finish(s0, v):
        rows = pl.ds(s0, LANES)
        gs = g[rows, lanes].astype(f32)
        dx[rows, lanes] = (v + gain * gs).astype(bf16)
        scr["direct"][...] += jnp.sum(
            (x[rows, lanes].astype(f32) * gs).reshape(LANES // 8, 8, LANES), axis=0
        )

    scr["direct"][...] = jnp.zeros_like(scr["direct"])
    if blocks <= 4:
        for i in range(blocks):
            s0 = i * LANES
            finish(s0, tile(pair, s0, s0, length - s0, True, x, g, scr))
    else:

        def block(i, _):
            s0 = pl.multiple_of(i * LANES, LANES)
            scr["vacc"][...] = tile(pair, s0, s0, LANES, True, x, g, scr)

            def right(j, _):
                t0 = pl.multiple_of(j * LANES, LANES)
                scr["vacc"][...] += tile(pair, s0, t0, LANES, False, x, g, scr)
                return 0

            lax.fori_loop(i + 1, blocks, right, 0)
            finish(s0, scr["vacc"][...])
            return 0

        lax.fori_loop(0, blocks, block, 0)
    direct = jnp.sum(scr["direct"][...], axis=0, keepdims=True)
    for k in range(2):
        scr["row"][pl.ds(2 * pair + k, 1), :] = jnp.sum(scr["racc"][k], axis=0, keepdims=True)
        mine = jnp.where(low, direct, 0.0) if k == 0 else jnp.where(low, 0.0, direct)
        scr["gain"][pl.ds(2 * pair + k, 1), :] = jnp.broadcast_to(
            jnp.sum(mine, axis=1, keepdims=True), (1, LANES)
        )


def scores(bk, ck, scr, length):
    blocks = length // LANES
    for i in range(blocks):
        s0 = i * LANES
        scr["score"][s0 : s0 + LANES, s0:] = dot_nt(bk[s0 : s0 + LANES, :], ck[s0:, :])
        scr["q"][s0 : s0 + LANES, s0:] = jnp.zeros((LANES, length - s0), f32)


def step_grads(scr, heads, length):
    col = scr["col"][...].T[:heads]
    dl = scan_lanes(scr["row"][...] - col, True)
    rate = scr["rate"][:, :1]
    dt = scr["dts"][...]
    ddt = col / dt - rate * dl
    draw = ddt * scr["sig"][...]
    pad = jnp.zeros((LANES - heads, length), f32)
    step = jnp.concatenate([draw, pad], axis=0).T
    decay = -rate * jnp.sum(dl * dt, axis=1, keepdims=True)
    shift = jnp.sum(draw, axis=1, keepdims=True)
    lane = iota((heads, LANES), 1)
    params = jnp.where(lane == 0, decay, jnp.where(lane == 1, scr["gain"][...], shift))
    params = jnp.concatenate([params, jnp.zeros((LANES - heads, LANES), f32)], axis=0).T
    return step[:, :heads], params[:3, :heads]


def key_grads(bk, ck, scr, length, write):
    blocks = length // LANES
    bt = bk[...].astype(f32).T.astype(bf16)
    for i in range(blocks):
        here = slice(i * LANES, (i + 1) * LANES)
        hi, lo = split_two(scr["q"][here, i * LANES :])
        db = dot_nn(hi, ck[i * LANES :, :]) + dot_nn(lo, ck[i * LANES :, :])
        upto = (i + 1) * LANES
        hi, lo = split_two(scr["q"][:upto, here])
        dc = dot_nn(bt[:, :upto], hi) + dot_nn(bt[:, :upto], lo)
        write(i, db, dc.T)


def scratch(heads, length):
    width = length if length <= 4 * LANES else LANES
    return {
        "wide": pltpu.VMEM((length, LANES), f32),
        "small": pltpu.VMEM((8, LANES), f32),
        "arow": pltpu.VMEM((heads, 8, length), f32),
        "acol": pltpu.VMEM((heads, length, LANES), f32),
        "dts": pltpu.VMEM((heads, length), f32),
        "sig": pltpu.VMEM((heads, length), f32),
        "rate": pltpu.VMEM((heads, LANES), f32),
        "score": pltpu.VMEM((length, length), f32),
        "q": pltpu.VMEM((length, length), f32),
        "col": pltpu.VMEM((length, LANES), f32),
        "row": pltpu.VMEM((heads, length), f32),
        "gain": pltpu.VMEM((heads, LANES), f32),
        "racc": pltpu.VMEM((2, 8, length), f32),
        "direct": pltpu.VMEM((8, LANES), f32),
        "vacc": pltpu.VMEM((LANES, LANES), f32),
        "w": pltpu.VMEM((2, LANES, width), f32),
        "m": pltpu.VMEM((4, LANES, width), bf16),
    }


def kernel(names, heads, length, x, raw, bk, ck, g, decay, skip, bias, dx, step, dkeys, par, *rest):
    scr = dict(zip(names, rest))
    prepare(
        raw, decay, bias, scr["wide"], scr["small"], scr["arow"], scr["acol"],
        scr["dts"], scr["sig"], scr["rate"], heads,
    )
    scores(bk, ck, scr, length)
    scr["col"][...] = jnp.zeros_like(scr["col"])

    def body(pair, _):
        one_pair(pair, x, g, skip, dx, scr, length)
        return 0

    lax.fori_loop(0, heads // 2, body, 0)
    step_out, par_out = step_grads(scr, heads, length)
    step[...] = step_out.astype(bf16)
    par[...] = par_out

    def write(i, db, dc):
        rows = slice(i * LANES, (i + 1) * LANES)
        dkeys[rows, :LANES] = db
        dkeys[rows, LANES:] = dc

    key_grads(bk, ck, scr, length, write)


def backward(x, raw, bk, ck, g, decay, skip, bias):
    length, heads = raw.shape
    space = scratch(heads, length)
    vmem = pl.BlockSpec(memory_space=pltpu.VMEM)
    smem = pl.BlockSpec(memory_space=pltpu.SMEM)
    return pl.pallas_call(
        functools.partial(kernel, tuple(space), heads, length),
        out_shape=(
            jax.ShapeDtypeStruct(x.shape, bf16),
            jax.ShapeDtypeStruct(raw.shape, bf16),
            jax.ShapeDtypeStruct((length, 2 * LANES), f32),
            jax.ShapeDtypeStruct((3, heads), f32),
        ),
        in_specs=[vmem, vmem, vmem, vmem, vmem, vmem, smem, vmem],
        out_specs=(vmem, vmem, vmem, vmem),
        scratch_shapes=list(space.values()),
        compiler_params=pltpu.CompilerParams(vmem_limit_bytes=60 * 1024 * 1024),
    )(x, raw, bk, ck, g, decay.reshape(1, heads), skip, bias.reshape(1, heads))


def shards(inputs, raw_step, write_keys, read_keys, grad_out, decay_log, skip_gain, step_bias):
    replicas = lax.axis_size("dp")
    swap = functools.partial(lax.all_to_all, axis_name="seq", split_axis=1, concat_axis=0, tiled=True)
    x, g, raw = swap(inputs[0]), swap(grad_out[0]), swap(raw_step[0])
    keys = lax.all_gather(jnp.concatenate([write_keys[0], read_keys[0]], axis=1), "seq", axis=0, tiled=True)
    dx, step, dkeys, par = backward(
        x, raw, keys[:, :LANES], keys[:, LANES:], g, decay_log, skip_gain, step_bias
    )
    back = functools.partial(lax.all_to_all, axis_name="seq", split_axis=0, concat_axis=1, tiled=True)
    grad_x, grad_step = back(dx), back(step)
    summed = lax.psum_scatter(dkeys, "seq", scatter_dimension=0, tiled=True).astype(bf16)
    total = lax.psum(par, "dp") / replicas
    return (
        grad_x[None], grad_step[None], summed[None, :, :LANES], summed[None, :, LANES:], total,
    )


def solution(mesh):
    rows = P("dp", "seq", None)
    return jax.shard_map(
        shards,
        mesh=mesh,
        in_specs=(rows,) * 5 + (P("seq"),) * 3,
        out_specs=(rows,) * 4 + (P(None, "seq"),),
        check_vma=False,
    )
```

```python
import functools

import jax
import jax.numpy as jnp
from jax import lax
from jax.experimental import pallas as pl
from jax.experimental.pallas import tpu as pltpu
from jax.sharding import PartitionSpec as P

LANES = 128
ROWS = 16
LOG2E = 1.4426950408889634
bf16 = jnp.bfloat16
f32 = jnp.float32


def iota(shape, dim):
    return lax.broadcasted_iota(jnp.int32, shape, dim)


def dot_nt(a, b):
    return lax.dot_general(a, b, (((1,), (1,)), ((), ())), preferred_element_type=f32)


def dot_nn(a, b):
    return jnp.dot(a, b, preferred_element_type=f32)


def split_two(v):
    hi = v.astype(bf16)
    return hi, (v - hi.astype(f32)).astype(bf16)


def scan_lanes(v, reverse):
    rows, length = v.shape
    width = min(256, length)
    r, c = iota((width, width), 0), iota((width, width), 1)
    keep = (r >= c) if reverse else (r <= c)
    ones = jnp.where(keep, 1.0, 0.0).astype(bf16)
    one = v.astype(bf16)
    rest = v - one.astype(f32)
    two = rest.astype(bf16)
    three = (rest - two.astype(f32)).astype(bf16)
    stacked = jnp.concatenate([one, two, three], axis=0)
    spots = list(range(0, length, width))
    carry = jnp.zeros((rows, 1), f32)
    out = {}
    for start in reversed(spots) if reverse else spots:
        part = dot_nn(stacked[:, start : start + width], ones)
        part = part[:rows] + (part[rows : 2 * rows] + part[2 * rows :]) + carry
        out[start] = part
        carry = part[:, :1] if reverse else part[:, width - 1 :]
    return jnp.concatenate([out[s] for s in spots], axis=1)


def prepare(raw, offset, decay, bias, wide, small, arow, acol, dts, sig, rate, heads):
    length, total = raw.shape
    pick = jnp.where(iota((total, LANES), 0) == iota((total, LANES), 1) + offset, 1.0, 0.0)
    small[...] = jnp.zeros_like(small)
    small[1:2, :heads] = bias[...]
    wide[...] = dot_nn(raw[...], pick.astype(bf16)) + small[1:2, :]
    z = wide[...].T[:heads]
    small[0:1, :heads] = jnp.exp(decay[...])
    rate_col = jnp.broadcast_to(small[0:1, :], (LANES, LANES)).T[:heads]
    rate[...] = rate_col
    dt = jnp.maximum(z, 0.0) + jnp.log1p(jnp.exp(-jnp.abs(z)))
    dts[...] = dt
    sig[...] = 1.0 / (1.0 + jnp.exp(-z))
    a = scan_lanes(dt * (rate_col[:, :1] * -LOG2E), False)
    for h in range(heads):
        arow[h] = jnp.broadcast_to(a[h : h + 1, :], (8, length))
    below = a - jnp.log(dt) * LOG2E
    column = jnp.concatenate([below, jnp.zeros((LANES - heads, length), f32)], axis=0).T
    for h in range(heads):
        acol[h] = jnp.broadcast_to(column[:, h : h + 1], (length, LANES))


def tile(pair, s0, t0, width, diagonal, x, g, scr):
    w, m, vacc = scr["w"], scr["m"], scr["vacc"]
    lanes = pl.ds(pl.multiple_of(pair * LANES, LANES), LANES)
    srows, trows = pl.ds(s0, LANES), pl.ds(t0, width)
    xs = x[srows, lanes]
    gs = g[trows, lanes]
    low = iota((width, LANES), 1) < LANES // 2
    zero = jnp.zeros_like(gs)
    parts = (jnp.where(low, gs, zero), jnp.where(low, zero, gs))
    for k in range(2):
        w[k, :, :width] = dot_nt(xs, parts[k])
    lane = iota((ROWS, LANES), 1)
    at = [scr["arow"][2 * pair + k, :, trows] for k in range(2)]
    at = [jnp.concatenate([v] * (ROWS // 8), axis=0) for v in at]
    sums = [None, None]
    for c in range(LANES // ROWS):
        rows = pl.ds(s0 + c * ROWS, ROWS)
        here = slice(c * ROWS, (c + 1) * ROWS)
        s_tile = scr["score"][rows, trows]
        q = scr["q"][rows, trows]
        col = scr["col"][rows, :]
        for k in range(2):
            ac = scr["acol"][2 * pair + k, rows, :]
            gap = at[k] - jnp.concatenate([ac] * (width // LANES), axis=1)
            if diagonal:
                keep = iota((ROWS, width), 1) >= iota((ROWS, width), 0) + c * ROWS
                gap = jnp.where(keep, gap, -jnp.inf)
            lp = jnp.exp2(gap)
            wk = w[k, here, :width]
            q = q + lp * wk
            mk = lp * s_tile
            hi, lo = split_two(mk)
            m[2 * k, here, :width] = hi
            m[2 * k + 1, here, :width] = lo
            zk = mk * wk
            part = zk[:8] + zk[8:]
            sums[k] = part if sums[k] is None else sums[k] + part
            across = zk[:, :LANES]
            for j in range(1, width // LANES):
                across = across + zk[:, j * LANES : (j + 1) * LANES]
            total = jnp.sum(across, axis=1, keepdims=True)
            col = col + jnp.where(lane == 2 * pair + k, total, 0.0)
        scr["q"][rows, trows] = q
        scr["col"][rows, :] = col
    for k in range(2):
        scr["racc"][k, :, trows] += sums[k]
    v = None
    for k in range(2):
        for j in range(2):
            term = dot_nn(m[2 * k + j, :, :width], parts[k])
            v = term if v is None else v + term
    return v


def one_pair(pair, x, g, skip, dx, scr, length):
    lanes = pl.ds(pl.multiple_of(pair * LANES, LANES), LANES)
    scr["racc"][...] = jnp.zeros_like(scr["racc"])
    low = iota((1, LANES), 1) < LANES // 2
    gain = jnp.where(low, skip[2 * pair], skip[2 * pair + 1])
    blocks = length // LANES

    def finish(s0, v):
        rows = pl.ds(s0, LANES)
        gs = g[rows, lanes].astype(f32)
        dx[rows, lanes] = (v + gain * gs).astype(bf16)
        scr["direct"][...] += jnp.sum(
            (x[rows, lanes].astype(f32) * gs).reshape(LANES // 8, 8, LANES), axis=0
        )

    scr["direct"][...] = jnp.zeros_like(scr["direct"])
    if blocks <= 4:
        for i in range(blocks):
            s0 = i * LANES
            finish(s0, tile(pair, s0, s0, length - s0, True, x, g, scr))
    else:

        def block(i, _):
            s0 = pl.multiple_of(i * LANES, LANES)
            scr["vacc"][...] = tile(pair, s0, s0, LANES, True, x, g, scr)

            def right(j, _):
                t0 = pl.multiple_of(j * LANES, LANES)
                scr["vacc"][...] += tile(pair, s0, t0, LANES, False, x, g, scr)
                return 0

            lax.fori_loop(i + 1, blocks, right, 0)
            finish(s0, scr["vacc"][...])
            return 0

        lax.fori_loop(0, blocks, block, 0)
    direct = jnp.sum(scr["direct"][...], axis=0, keepdims=True)
    for k in range(2):
        scr["row"][pl.ds(2 * pair + k, 1), :] = jnp.sum(scr["racc"][k], axis=0, keepdims=True)
        mine = jnp.where(low, direct, 0.0) if k == 0 else jnp.where(low, 0.0, direct)
        scr["gain"][pl.ds(2 * pair + k, 1), :] = jnp.broadcast_to(
            jnp.sum(mine, axis=1, keepdims=True), (1, LANES)
        )


def scores(bk, ck, scr, length):
    blocks = length // LANES
    for i in range(blocks):
        s0 = i * LANES
        scr["score"][s0 : s0 + LANES, s0:] = dot_nt(bk[s0 : s0 + LANES, :], ck[s0:, :])
        scr["q"][s0 : s0 + LANES, s0:] = jnp.zeros((LANES, length - s0), f32)


def step_grads(scr, heads, length):
    col = scr["col"][...].T[:heads]
    dl = scan_lanes(scr["row"][...] - col, True)
    rate = scr["rate"][:, :1]
    dt = scr["dts"][...]
    ddt = col / dt - rate * dl
    draw = ddt * scr["sig"][...]
    pad = jnp.zeros((LANES - heads, length), f32)
    step = jnp.concatenate([draw, pad], axis=0).T
    decay = -rate * jnp.sum(dl * dt, axis=1, keepdims=True)
    shift = jnp.sum(draw, axis=1, keepdims=True)
    lane = iota((heads, LANES), 1)
    params = jnp.where(lane == 0, decay, jnp.where(lane == 1, scr["gain"][...], shift))
    params = jnp.concatenate([params, jnp.zeros((LANES - heads, LANES), f32)], axis=0).T
    return step, params[:8]


def key_grads(bk, ck, scr, length, write):
    blocks = length // LANES
    bt = bk[...].astype(f32).T.astype(bf16)
    for i in range(blocks):
        here = slice(i * LANES, (i + 1) * LANES)
        hi, lo = split_two(scr["q"][here, i * LANES :])
        db = dot_nn(hi, ck[i * LANES :, :]) + dot_nn(lo, ck[i * LANES :, :])
        upto = (i + 1) * LANES
        hi, lo = split_two(scr["q"][:upto, here])
        dc = dot_nn(bt[:, :upto], hi) + dot_nn(bt[:, :upto], lo)
        write(i, db, dc.T)


def scratch(heads, length):
    width = length if length <= 4 * LANES else LANES
    return {
        "wide": pltpu.VMEM((length, LANES), f32),
        "small": pltpu.VMEM((8, LANES), f32),
        "arow": pltpu.VMEM((heads, 8, length), f32),
        "acol": pltpu.VMEM((heads, length, LANES), f32),
        "dts": pltpu.VMEM((heads, length), f32),
        "sig": pltpu.VMEM((heads, length), f32),
        "rate": pltpu.VMEM((heads, LANES), f32),
        "score": pltpu.VMEM((length, length), f32),
        "q": pltpu.VMEM((length, length), f32),
        "col": pltpu.VMEM((length, LANES), f32),
        "row": pltpu.VMEM((heads, length), f32),
        "gain": pltpu.VMEM((heads, LANES), f32),
        "racc": pltpu.VMEM((2, 8, length), f32),
        "direct": pltpu.VMEM((8, LANES), f32),
        "vacc": pltpu.VMEM((LANES, LANES), f32),
        "w": pltpu.VMEM((2, LANES, width), f32),
        "m": pltpu.VMEM((4, LANES, width), bf16),
    }


def kernel(names, n, replicas, x_hbm, raw, wk, rk, g_hbm, decay, skip, bias, dx_out, step, dwrite, dread, par, *rest):
    scr = dict(zip(names, rest))
    rows = x_hbm.shape[0]
    length = rows * n
    heads = decay.shape[1]
    pairs = heads // 2
    span = pairs * LANES
    me, dp = lax.axis_index("seq"), lax.axis_index("dp")
    x, g, dx, bk, ck, raws = (scr[k] for k in ("x", "g", "dx", "bk", "ck", "raws"))
    mine = pl.ds(pl.multiple_of(me * rows, rows), rows)
    left = pl.ds(pl.multiple_of(me * span, span), span)

    def seq(k):
        return lax.rem(me + k, n)

    def replica(k):
        return lax.rem(dp + k, replicas)

    def send(src, dst, out_sem, in_sem, target):
        return pltpu.make_async_remote_copy(
            src_ref=src, dst_ref=dst, send_sem=out_sem, recv_sem=in_sem,
            device_id=target, device_id_type=pl.DeviceIdType.MESH,
        )

    order = [k for k in range(1, n)]

    barrier = pltpu.get_barrier_semaphore()
    for k in range(1, n):
        pl.semaphore_signal(barrier, inc=1, device_id={"seq": seq(k)}, device_id_type=pl.DeviceIdType.MESH)
    for k in range(1, replicas):
        pl.semaphore_signal(barrier, inc=1, device_id={"dp": replica(k)}, device_id_type=pl.DeviceIdType.MESH)
    own = [
        pltpu.make_async_copy(x_hbm.at[:, left], x.at[mine, :], scr["own"].at[0]),
        pltpu.make_async_copy(g_hbm.at[:, left], g.at[mine, :], scr["own"].at[1]),
    ]
    for copy in own:
        copy.start()
    bk[mine, :] = wk[...]
    ck[mine, :] = rk[...]
    raws[mine, :] = raw[...]
    pl.semaphore_wait(barrier, n + replicas - 2)

    def key_copies(k):
        target = {"seq": seq(k)}
        return [
            send(src, dst.at[mine, :], scr["key_out"].at[k, j], scr["key_in"].at[k, j], target)
            for j, (src, dst) in enumerate(((wk, bk), (rk, ck), (raw, raws)))
        ]

    def entry_copies(p, k):
        target = seq(k)
        there = pl.ds(pl.multiple_of(target * span + p * LANES, LANES), LANES)
        here = pl.ds(pl.multiple_of(p * LANES, LANES), LANES)
        return [
            send(
                src.at[:, there], dst.at[mine, here], scr["go_out"].at[p, k, j],
                scr["go_in"].at[p, k, j], {"seq": target},
            )
            for j, (src, dst) in enumerate(((x_hbm, x), (g_hbm, g)))
        ]

    def exit_copy(p, k):
        target = seq(k)
        theirs = pl.ds(pl.multiple_of(target * rows, rows), rows)
        here = pl.ds(pl.multiple_of(p * LANES, LANES), LANES)
        there = pl.ds(pl.multiple_of(me * span + p * LANES, LANES), LANES)
        return send(
            dx.at[theirs, here], dx_out.at[:, there], scr["back_out"].at[p, k],
            scr["back_in"].at[p, k], {"seq": target},
        )

    for k in order:
        for copy in key_copies(k):
            copy.start()

    def launch(p, _):
        for k in order:
            for copy in entry_copies(p, k):
                copy.start()
        return 0

    lax.fori_loop(0, pairs, launch, 0)
    for k in order:
        for copy in key_copies(k):
            copy.wait_recv()
    prepare(
        raws, me * heads, decay, bias, scr["wide"], scr["small"], scr["arow"], scr["acol"],
        scr["dts"], scr["sig"], scr["rate"], heads,
    )
    scores(bk, ck, scr, length)
    scr["col"][...] = jnp.zeros_like(scr["col"])
    for copy in own:
        copy.wait()

    def body(p, _):
        for k in order:
            for copy in entry_copies(p, k):
                copy.wait_recv()
        one_pair(p, x, g, skip, dx, scr, length)
        for k in order:
            exit_copy(p, k).start()
        return 0

    lax.fori_loop(0, pairs, body, 0)
    keep = pltpu.make_async_copy(dx.at[mine, :], dx_out.at[:, left], scr["own"].at[2])
    keep.start()

    def write(i, db, dc):
        here = slice(i * LANES, (i + 1) * LANES)
        scr["dkeys"][here, :LANES] = db
        scr["dkeys"][here, LANES:] = dc

    key_grads(bk, ck, scr, length, write)

    def sum_copy(k):
        theirs = pl.ds(pl.multiple_of(seq(k) * rows, rows), rows)
        return send(
            scr["dkeys"].at[theirs, :], scr["dk_got"].at[k], scr["dk_out"].at[k],
            scr["dk_in"].at[k], {"seq": seq(k)},
        )

    for k in order:
        sum_copy(k).start()
    step_all, params = step_grads(scr, heads, length)
    place = jnp.where(iota((LANES, LANES), 0) + me * heads == iota((LANES, LANES), 1), 1.0, 0.0)
    place = jnp.where(iota((LANES, LANES), 0) < heads, place, 0.0)
    scr["step"][...] = dot_nn(step_all.astype(bf16), place.astype(bf16)).astype(bf16)
    scr["par"][...] = params

    def step_copy(k):
        theirs = pl.ds(pl.multiple_of(seq(k) * rows, rows), rows)
        return send(
            scr["step"].at[theirs, :], scr["step_got"].at[k], scr["st_out"].at[k],
            scr["st_in"].at[k], {"seq": seq(k)},
        )

    def par_copy(k):
        return send(
            scr["par"], scr["par_got"].at[k], scr["par_out"].at[k], scr["par_in"].at[k],
            {"dp": replica(k)},
        )

    for k in range(1, replicas):
        par_copy(k).start()
    for k in order:
        step_copy(k).start()

    total = scr["dkeys"][mine, :]
    for k in order:
        sum_copy(k).wait_recv()
        total = total + scr["dk_got"][k]
    dwrite[...] = total[:, :LANES].astype(bf16)
    dread[...] = total[:, LANES:].astype(bf16)
    steps = scr["step"][mine, :].astype(f32)
    for k in order:
        step_copy(k).wait_recv()
        steps = steps + scr["step_got"][k].astype(f32)
    step[...] = steps[:, : step.shape[1]].astype(bf16)
    params = scr["par"][...]
    for k in range(1, replicas):
        par_copy(k).wait_recv()
        params = params + scr["par_got"][k]
    par[...] = params[:3, :heads] / replicas

    keep.wait()

    def drain(p, _):
        for k in order:
            for copy in entry_copies(p, k):
                copy.wait_send()
            exit_copy(p, k).wait()
        return 0

    lax.fori_loop(0, pairs, drain, 0)
    for k in order:
        for copy in key_copies(k):
            copy.wait_send()
        sum_copy(k).wait_send()
        step_copy(k).wait_send()
    for k in range(1, replicas):
        par_copy(k).wait_send()


def backward(n, replicas, x, raw, wk, rk, g, decay, skip, bias):
    rows, total = raw.shape
    heads, length = decay.shape[0], rows * n
    pairs = heads // 2
    dma = pltpu.SemaphoreType.DMA
    space = scratch(heads, length) | {
        "x": pltpu.VMEM((length, pairs * LANES), bf16),
        "g": pltpu.VMEM((length, pairs * LANES), bf16),
        "dx": pltpu.VMEM((length, pairs * LANES), bf16),
        "bk": pltpu.VMEM((length, LANES), bf16),
        "ck": pltpu.VMEM((length, LANES), bf16),
        "raws": pltpu.VMEM((length, total), bf16),
        "dkeys": pltpu.VMEM((length, 2 * LANES), f32),
        "dk_got": pltpu.VMEM((n, rows, 2 * LANES), f32),
        "step": pltpu.VMEM((length, LANES), bf16),
        "step_got": pltpu.VMEM((n, rows, LANES), bf16),
        "par": pltpu.VMEM((8, LANES), f32),
        "par_got": pltpu.VMEM((replicas, 8, LANES), f32),
        "own": dma((3,)),
        "key_out": dma((n, 3)),
        "key_in": dma((n, 3)),
        "go_out": dma((pairs, n, 2)),
        "go_in": dma((pairs, n, 2)),
        "back_out": dma((pairs, n)),
        "back_in": dma((pairs, n)),
        "dk_out": dma((n,)),
        "dk_in": dma((n,)),
        "st_out": dma((n,)),
        "st_in": dma((n,)),
        "par_out": dma((replicas,)),
        "par_in": dma((replicas,)),
    }
    vmem = pl.BlockSpec(memory_space=pltpu.VMEM)
    smem = pl.BlockSpec(memory_space=pltpu.SMEM)
    hbm = pl.BlockSpec(memory_space=pl.ANY)
    return pl.pallas_call(
        functools.partial(kernel, tuple(space), n, replicas),
        out_shape=(
            jax.ShapeDtypeStruct(x.shape, bf16),
            jax.ShapeDtypeStruct(raw.shape, bf16),
            jax.ShapeDtypeStruct(wk.shape, bf16),
            jax.ShapeDtypeStruct(rk.shape, bf16),
            jax.ShapeDtypeStruct((3, heads), f32),
        ),
        in_specs=[hbm, vmem, vmem, vmem, hbm, vmem, smem, vmem],
        out_specs=(hbm, vmem, vmem, vmem, vmem),
        scratch_shapes=list(space.values()),
        compiler_params=pltpu.CompilerParams(
            vmem_limit_bytes=60 * 1024 * 1024, collective_id=0, has_side_effects=True
        ),
    )(x, raw, wk, rk, g, decay.reshape(1, heads), skip, bias.reshape(1, heads))


def shards(n, replicas, inputs, raw_step, write_keys, read_keys, grad_out, decay_log, skip_gain, step_bias):
    dx, step, dwrite, dread, par = backward(
        n, replicas, inputs[0], raw_step[0], write_keys[0], read_keys[0], grad_out[0],
        decay_log, skip_gain, step_bias,
    )
    return dx[None], step[None], dwrite[None], dread[None], par


def solution(mesh):
    rows = P("dp", "seq", None)
    return jax.shard_map(
        functools.partial(shards, mesh.shape["seq"], mesh.shape["dp"]),
        mesh=mesh,
        in_specs=(rows,) * 5 + (P("seq"),) * 3,
        out_specs=(rows,) * 4 + (P(None, "seq"),),
        check_vma=False,
    )
```

```python
import functools
import types

import jax
import jax.numpy as jnp
from jax import lax
from jax.experimental import pallas as pl
from jax.experimental.pallas import tpu as pltpu
from jax.sharding import PartitionSpec as P

LANES = 128
ROWS = 16
LOG2E = 1.4426950408889634
bf16 = jnp.bfloat16
f32 = jnp.float32


def iota(shape, dim):
    return lax.broadcasted_iota(jnp.int32, shape, dim)


def dot_nt(a, b):
    return lax.dot_general(a, b, (((1,), (1,)), ((), ())), preferred_element_type=f32)


def dot_nn(a, b):
    return jnp.dot(a, b, preferred_element_type=f32)


def split_two(v):
    hi = v.astype(bf16)
    return hi, (v - hi.astype(f32)).astype(bf16)


def scan_lanes(v, reverse):
    rows, length = v.shape
    width = min(256, length)
    r, c = iota((width, width), 0), iota((width, width), 1)
    keep = (r >= c) if reverse else (r <= c)
    ones = jnp.where(keep, 1.0, 0.0).astype(bf16)
    one = v.astype(bf16)
    rest = v - one.astype(f32)
    two = rest.astype(bf16)
    three = (rest - two.astype(f32)).astype(bf16)
    stacked = jnp.concatenate([one, two, three], axis=0)
    spots = list(range(0, length, width))
    carry = jnp.zeros((rows, 1), f32)
    out = {}
    for start in reversed(spots) if reverse else spots:
        part = dot_nn(stacked[:, start : start + width], ones)
        part = part[:rows] + (part[rows : 2 * rows] + part[2 * rows :]) + carry
        out[start] = part
        carry = part[:, :1] if reverse else part[:, width - 1 :]
    return jnp.concatenate([out[s] for s in spots], axis=1)


def column(small, row, heads):
    small[0:1, :heads] = row
    return jnp.broadcast_to(small[0:1, :], (LANES, LANES)).T[:heads]


def pick_heads(raws, offset, heads):
    n, total, _ = raws.shape
    pick = jnp.where(iota((heads, total), 1) == iota((heads, total), 0) + offset, 1.0, 0.0)
    return jnp.concatenate([dot_nn(pick.astype(bf16), raws[k]) for k in range(n)], axis=1)


def prepare(z, decay, bias, small, arow, acol, dts, sig, rate, heads):
    length = z.shape[1]
    small[...] = jnp.zeros_like(small)
    z = z + column(small, bias, heads)[:, :1]
    rate_col = column(small, jnp.exp(decay), heads)
    rate[...] = rate_col
    dt = jnp.maximum(z, 0.0) + jnp.log1p(jnp.exp(-jnp.abs(z)))
    dts[...] = dt
    sig[...] = 1.0 / (1.0 + jnp.exp(-z))
    a = scan_lanes(dt * (rate_col[:, :1] * -LOG2E), False)
    for h in range(heads):
        arow[h] = jnp.broadcast_to(a[h : h + 1, :], (8, length))
    below = a - jnp.log(dt) * LOG2E
    down = jnp.concatenate([below, jnp.zeros((LANES - heads, length), f32)], axis=0).T
    for h in range(heads):
        acol[h] = jnp.broadcast_to(down[:, h : h + 1], (length, LANES))


def tile(pair, s0, t0, width, diagonal, x, g, scr):
    w, m, vacc = scr.w, scr.m, scr.vacc
    lanes = pl.ds(pl.multiple_of(pair * LANES, LANES), LANES)
    srows, trows = pl.ds(s0, LANES), pl.ds(t0, width)
    xs = x[srows, lanes]
    gs = g[trows, lanes]
    low = iota((width, LANES), 1) < LANES // 2
    zero = jnp.zeros_like(gs)
    parts = (jnp.where(low, gs, zero), jnp.where(low, zero, gs))
    for k in range(2):
        w[k, :, :width] = dot_nt(xs, parts[k])
    lane = iota((ROWS, LANES), 1)
    at = [scr.arow[2 * pair + k, :, trows] for k in range(2)]
    at = [jnp.concatenate([v] * (ROWS // 8), axis=0) for v in at]
    sums = [None, None]
    for c in range(LANES // ROWS):
        rows = pl.ds(s0 + c * ROWS, ROWS)
        here = slice(c * ROWS, (c + 1) * ROWS)
        s_tile = scr.score[rows, trows]
        q = scr.q[rows, trows]
        col = scr.col[rows, :]
        for k in range(2):
            ac = scr.acol[2 * pair + k, rows, :]
            gap = at[k] - jnp.concatenate([ac] * (width // LANES), axis=1)
            if diagonal:
                keep = iota((ROWS, width), 1) >= iota((ROWS, width), 0) + c * ROWS
                gap = jnp.where(keep, gap, -jnp.inf)
            lp = jnp.exp2(gap)
            wk = w[k, here, :width]
            q = q + lp * wk
            mk = lp * s_tile
            hi, lo = split_two(mk)
            m[2 * k, here, :width] = hi
            m[2 * k + 1, here, :width] = lo
            zk = mk * wk
            part = zk[:8] + zk[8:]
            sums[k] = part if sums[k] is None else sums[k] + part
            across = zk[:, :LANES]
            for j in range(1, width // LANES):
                across = across + zk[:, j * LANES : (j + 1) * LANES]
            total = jnp.sum(across, axis=1, keepdims=True)
            col = col + jnp.where(lane == 2 * pair + k, total, 0.0)
        scr.q[rows, trows] = q
        scr.col[rows, :] = col
    for k in range(2):
        scr.racc[k, :, trows] += sums[k]
    v = None
    for k in range(2):
        for j in range(2):
            term = dot_nn(m[2 * k + j, :, :width], parts[k])
            v = term if v is None else v + term
    return v


def one_pair(pair, x, g, gain, dx, scr, length):
    lanes = pl.ds(pl.multiple_of(pair * LANES, LANES), LANES)
    scr.racc[...] = jnp.zeros_like(scr.racc)
    low = iota((1, LANES), 1) < LANES // 2
    blocks = length // LANES

    def finish(s0, v):
        rows = pl.ds(s0, LANES)
        gs = g[rows, lanes].astype(f32)
        dx[rows, lanes] = (v + gain * gs).astype(dx.dtype)
        scr.direct[...] += jnp.sum(
            (x[rows, lanes].astype(f32) * gs).reshape(LANES // 8, 8, LANES), axis=0
        )

    scr.direct[...] = jnp.zeros_like(scr.direct)
    if blocks <= 4:
        for i in range(blocks):
            s0 = i * LANES
            finish(s0, tile(pair, s0, s0, length - s0, True, x, g, scr))
    else:

        def block(i, _):
            s0 = pl.multiple_of(i * LANES, LANES)
            scr.vacc[...] = tile(pair, s0, s0, LANES, True, x, g, scr)

            def right(j, _):
                t0 = pl.multiple_of(j * LANES, LANES)
                scr.vacc[...] += tile(pair, s0, t0, LANES, False, x, g, scr)
                return 0

            lax.fori_loop(i + 1, blocks, right, 0)
            finish(s0, scr.vacc[...])
            return 0

        lax.fori_loop(0, blocks, block, 0)
    direct = jnp.sum(scr.direct[...], axis=0, keepdims=True)
    for k in range(2):
        scr.row[pl.ds(2 * pair + k, 1), :] = jnp.sum(scr.racc[k], axis=0, keepdims=True)
        mine = jnp.where(low, direct, 0.0) if k == 0 else jnp.where(low, 0.0, direct)
        scr.gain[pl.ds(2 * pair + k, 1), :] = jnp.broadcast_to(
            jnp.sum(mine, axis=1, keepdims=True), (1, LANES)
        )


def scores(bk, ck, scr, length):
    blocks = length // LANES
    for i in range(blocks):
        s0 = i * LANES
        scr.score[s0 : s0 + LANES, s0:] = dot_nt(bk[s0 : s0 + LANES, :], ck[s0:, :])
        scr.q[s0 : s0 + LANES, s0:] = jnp.zeros((LANES, length - s0), f32)


def step_grads(scr, heads, length, cross=None):
    col = scr.col[...].T[:heads]
    row = scr.row[...]
    extra = 0.0
    if cross is not None:
        first, value = cross
        value = value.T[:heads]
        col = col + jnp.where(first, value, 0.0)
        row = row + jnp.where(first, 0.0, value)
        extra = jnp.where(first, jnp.sum(value, axis=1, keepdims=True), 0.0)
    dl = scan_lanes(row - col, True) + extra
    rate = scr.rate[:, :1]
    dt = scr.dts[...]
    ddt = col / dt - rate * dl
    draw = ddt * scr.sig[...]
    decay = -rate * jnp.sum(dl * dt, axis=1, keepdims=True)
    shift = jnp.sum(draw, axis=1, keepdims=True)
    lane = iota((heads, LANES), 1)
    params = jnp.where(lane == 0, decay, jnp.where(lane == 1, scr.gain[...], shift))
    params = jnp.concatenate([params, jnp.zeros((LANES - heads, LANES), f32)], axis=0).T
    return draw, params[:8]


def key_grads(bk, ck, scr, length, write):
    blocks = length // LANES
    bt = bk[...].astype(f32).T.astype(bf16)
    for i in range(blocks):
        here = slice(i * LANES, (i + 1) * LANES)
        hi, lo = split_two(scr.q[here, i * LANES :])
        db = dot_nn(hi, ck[i * LANES :, :]) + dot_nn(lo, ck[i * LANES :, :])
        upto = (i + 1) * LANES
        hi, lo = split_two(scr.q[:upto, here])
        dc = dot_nn(bt[:, :upto], hi) + dot_nn(bt[:, :upto], lo)
        write(i, db, dc.T)


def scratch(heads, length):
    width = length if length <= 4 * LANES else LANES
    return dict(
        small=pltpu.VMEM((8, LANES), f32),
        arow=pltpu.VMEM((heads, 8, length), f32),
        acol=pltpu.VMEM((heads, length, LANES), f32),
        dts=pltpu.VMEM((heads, length), f32),
        sig=pltpu.VMEM((heads, length), f32),
        rate=pltpu.VMEM((heads, LANES), f32),
        score=pltpu.VMEM((length, length), f32),
        q=pltpu.VMEM((length, length), f32),
        col=pltpu.VMEM((length, LANES), f32),
        row=pltpu.VMEM((heads, length), f32),
        gain=pltpu.VMEM((heads, LANES), f32),
        racc=pltpu.VMEM((2, 8, length), f32),
        direct=pltpu.VMEM((8, LANES), f32),
        vacc=pltpu.VMEM((LANES, LANES), f32),
        w=pltpu.VMEM((2, LANES, width), f32),
        m=pltpu.VMEM((4, LANES, width), bf16),
    )


def kernel(names, n, replicas, x_hbm, raw, wk, rk, g_hbm, decay, skip, bias, dx_out, step, dwrite, dread, par, *rest):
    scr = types.SimpleNamespace(**dict(zip(names, rest)))
    rows = x_hbm.shape[0]
    length = rows * n
    heads = decay.shape[1]
    pairs = heads // 2
    span = pairs * LANES
    me, dp = lax.axis_index("seq"), lax.axis_index("dp")
    x, g, dx, bk, ck, raws = (scr.x, scr.g, scr.dx, scr.bk, scr.ck, scr.raws)
    mine = pl.ds(pl.multiple_of(me * rows, rows), rows)
    left = pl.ds(pl.multiple_of(me * span, span), span)

    def seq(k):
        return lax.rem(me + k, n)

    def replica(k):
        return lax.rem(dp + k, replicas)

    def send(src, dst, out_sem, in_sem, target):
        return pltpu.make_async_remote_copy(
            src_ref=src, dst_ref=dst, send_sem=out_sem, recv_sem=in_sem,
            device_id=target, device_id_type=pl.DeviceIdType.MESH,
        )

    order = [k for k in range(1, n)]

    barrier = pltpu.get_barrier_semaphore()
    for k in range(1, n):
        pl.semaphore_signal(barrier, inc=1, device_id={"seq": seq(k)}, device_id_type=pl.DeviceIdType.MESH)
    for k in range(1, replicas):
        pl.semaphore_signal(barrier, inc=1, device_id={"dp": replica(k)}, device_id_type=pl.DeviceIdType.MESH)
    own = [
        pltpu.make_async_copy(x_hbm.at[:, left], x.at[mine, :], scr.own.at[0]),
        pltpu.make_async_copy(g_hbm.at[:, left], g.at[mine, :], scr.own.at[1]),
    ]
    for copy in own:
        copy.start()
    bk[mine, :] = wk[...]
    ck[mine, :] = rk[...]
    raws[me] = raw[...]
    pl.semaphore_wait(barrier, n + replicas - 2)

    def key_copies(k):
        target = {"seq": seq(k)}
        return [
            send(src, dst, scr.key_out.at[k, j], scr.key_in.at[k, j], target)
            for j, (src, dst) in enumerate(((wk, bk.at[mine, :]), (rk, ck.at[mine, :]), (raw, raws.at[me])))
        ]

    def entry_copies(p, k):
        target = seq(k)
        there = pl.ds(pl.multiple_of(target * span + p * LANES, LANES), LANES)
        here = pl.ds(pl.multiple_of(p * LANES, LANES), LANES)
        return [
            send(
                src.at[:, there], dst.at[mine, here], scr.go_out.at[p, k, j],
                scr.go_in.at[p, k, j], {"seq": target},
            )
            for j, (src, dst) in enumerate(((x_hbm, x), (g_hbm, g)))
        ]

    def exit_copy(p, k):
        target = seq(k)
        theirs = pl.ds(pl.multiple_of(target * rows, rows), rows)
        here = pl.ds(pl.multiple_of(p * LANES, LANES), LANES)
        there = pl.ds(pl.multiple_of(me * span + p * LANES, LANES), LANES)
        return send(
            dx.at[theirs, here], dx_out.at[:, there], scr.back_out.at[p, k],
            scr.back_in.at[p, k], {"seq": target},
        )

    for k in order:
        for copy in key_copies(k):
            copy.start()

    def launch(p, _):
        for k in order:
            for copy in entry_copies(p, k):
                copy.start()
        return 0

    lax.fori_loop(0, pairs, launch, 0)
    for k in order:
        for copy in key_copies(k):
            copy.wait_recv()
    prepare(
        pick_heads(raws, me * heads, heads), decay[...], bias[...], scr.small, scr.arow, scr.acol,
        scr.dts, scr.sig, scr.rate, heads,
    )
    scores(bk, ck, scr, length)
    scr.col[...] = jnp.zeros_like(scr.col)
    for copy in own:
        copy.wait()

    def body(p, _):
        for k in order:
            for copy in entry_copies(p, k):
                copy.wait_recv()
        low = iota((1, LANES), 1) < LANES // 2
        gain = jnp.where(low, skip[2 * p], skip[2 * p + 1])
        one_pair(p, x, g, gain, dx, scr, length)
        for k in order:
            exit_copy(p, k).start()
        return 0

    lax.fori_loop(0, pairs, body, 0)
    keep = pltpu.make_async_copy(dx.at[mine, :], dx_out.at[:, left], scr.own.at[2])
    keep.start()

    def write(i, db, dc):
        here = slice(i * LANES, (i + 1) * LANES)
        scr.dkeys[here, :LANES] = db
        scr.dkeys[here, LANES:] = dc

    key_grads(bk, ck, scr, length, write)

    def sum_copy(k):
        theirs = pl.ds(pl.multiple_of(seq(k) * rows, rows), rows)
        return send(
            scr.dkeys.at[theirs, :], scr.dk_got.at[k], scr.dk_out.at[k],
            scr.dk_in.at[k], {"seq": seq(k)},
        )

    for k in order:
        sum_copy(k).start()
    step_all, params = step_grads(scr, heads, length)
    spread = (raw.shape[0], heads)
    place = jnp.where(iota(spread, 1) + me * heads == iota(spread, 0), 1.0, 0.0)
    scr.step[...] = dot_nn(place.astype(bf16), step_all.astype(bf16)).astype(bf16)
    scr.par[...] = params

    def step_copy(k):
        theirs = pl.ds(pl.multiple_of(seq(k) * rows, rows), rows)
        return send(
            scr.step.at[:, theirs], scr.step_got.at[k], scr.st_out.at[k],
            scr.st_in.at[k], {"seq": seq(k)},
        )

    def par_copy(k):
        return send(
            scr.par, scr.par_got.at[k], scr.par_out.at[k], scr.par_in.at[k],
            {"dp": replica(k)},
        )

    for k in range(1, replicas):
        par_copy(k).start()
    for k in order:
        step_copy(k).start()

    total = scr.dkeys[mine, :]
    for k in order:
        sum_copy(k).wait_recv()
        total = total + scr.dk_got[k]
    dwrite[...] = total[:, :LANES].astype(bf16)
    dread[...] = total[:, LANES:].astype(bf16)
    steps = scr.step[:, mine].astype(f32)
    for k in order:
        step_copy(k).wait_recv()
        steps = steps + scr.step_got[k].astype(f32)
    step[...] = steps.astype(bf16)
    params = scr.par[...]
    for k in range(1, replicas):
        par_copy(k).wait_recv()
        params = params + scr.par_got[k]
    par[...] = params[:3, :heads] / replicas

    keep.wait()

    def drain(p, _):
        for k in order:
            for copy in entry_copies(p, k):
                copy.wait_send()
            exit_copy(p, k).wait()
        return 0

    lax.fori_loop(0, pairs, drain, 0)
    for k in order:
        for copy in key_copies(k):
            copy.wait_send()
        sum_copy(k).wait_send()
        step_copy(k).wait_send()
    for k in range(1, replicas):
        par_copy(k).wait_send()


def backward(n, replicas, x, raw, wk, rk, g, decay, skip, bias):
    total, rows = raw.shape
    heads, length = decay.shape[0], rows * n
    pairs = heads // 2
    dma = pltpu.SemaphoreType.DMA
    space = scratch(heads, length) | dict(
        x=pltpu.VMEM((length, pairs * LANES), bf16),
        g=pltpu.VMEM((length, pairs * LANES), bf16),
        dx=pltpu.VMEM((length, pairs * LANES), bf16),
        bk=pltpu.VMEM((length, LANES), bf16),
        ck=pltpu.VMEM((length, LANES), bf16),
        raws=pltpu.VMEM((length // rows, total, rows), bf16),
        dkeys=pltpu.VMEM((length, 2 * LANES), f32),
        dk_got=pltpu.VMEM((n, rows, 2 * LANES), f32),
        step=pltpu.VMEM((total, length), bf16),
        step_got=pltpu.VMEM((n, total, rows), bf16),
        par=pltpu.VMEM((8, LANES), f32),
        par_got=pltpu.VMEM((replicas, 8, LANES), f32),
        own=dma((3,)),
        key_out=dma((n, 3)),
        key_in=dma((n, 3)),
        go_out=dma((pairs, n, 2)),
        go_in=dma((pairs, n, 2)),
        back_out=dma((pairs, n)),
        back_in=dma((pairs, n)),
        dk_out=dma((n,)),
        dk_in=dma((n,)),
        st_out=dma((n,)),
        st_in=dma((n,)),
        par_out=dma((replicas,)),
        par_in=dma((replicas,)),
    )
    vmem = pl.BlockSpec(memory_space=pltpu.VMEM)
    smem = pl.BlockSpec(memory_space=pltpu.SMEM)
    hbm = pl.BlockSpec(memory_space=pl.ANY)
    return pl.pallas_call(
        functools.partial(kernel, tuple(space), n, replicas),
        out_shape=(
            jax.ShapeDtypeStruct(x.shape, bf16),
            jax.ShapeDtypeStruct(raw.shape, bf16),
            jax.ShapeDtypeStruct(wk.shape, bf16),
            jax.ShapeDtypeStruct(rk.shape, bf16),
            jax.ShapeDtypeStruct((3, heads), f32),
        ),
        in_specs=[hbm, vmem, vmem, vmem, hbm, vmem, smem, vmem],
        out_specs=(hbm, vmem, vmem, vmem, vmem),
        scratch_shapes=list(space.values()),
        compiler_params=pltpu.CompilerParams(
            vmem_limit_bytes=60 * 1024 * 1024, collective_id=0, has_side_effects=True
        ),
    )(x, raw, wk, rk, g, decay.reshape(1, heads), skip, bias.reshape(1, heads))


def chip_kernel(names, n, replicas, x_hbm, raw, wk, rk, g_hbm, decay, skip, bias, dx_out, step, dwrite, dread, par, *rest):
    scr = types.SimpleNamespace(**dict(zip(names, rest)))
    rows = x_hbm.shape[0]
    length = 2 * rows
    few = decay.shape[1]
    heads = 2 * few
    pairs = heads // 2
    span = pairs * LANES
    me, dp = lax.axis_index("seq"), lax.axis_index("dp")
    chip, core = me // 2, lax.rem(me, 2)
    first = chip == 0
    near, far = me + 1 - 2 * core, lax.rem(me + 2, n)
    x, g, bk, ck, raws = (scr.x, scr.g, scr.bk, scr.ck, scr.raws)
    dxf, dx = scr.dxf, scr.dx
    mine = pl.ds(pl.multiple_of(core * rows, rows), rows)
    theirs = pl.ds(pl.multiple_of((1 - core) * rows, rows), rows)
    left = pl.ds(pl.multiple_of(core * span, span), span)
    mesh_id = pl.DeviceIdType.MESH

    def seq(k):
        return lax.rem(me + k, n)

    def replica(k):
        return lax.rem(dp + k, replicas)

    def send(src, dst, name, at, target):
        return pltpu.make_async_remote_copy(
            src_ref=src, dst_ref=dst, send_sem=getattr(scr, name + "_out").at[at],
            recv_sem=getattr(scr, name + "_in").at[at], device_id=target, device_id_type=mesh_id,
        )

    barrier = pltpu.get_barrier_semaphore()
    for k in range(1, n):
        pl.semaphore_signal(barrier, inc=1, device_id={"seq": seq(k)}, device_id_type=mesh_id)
    for k in range(1, replicas):
        pl.semaphore_signal(barrier, inc=1, device_id={"dp": replica(k)}, device_id_type=mesh_id)
    own = [
        pltpu.make_async_copy(x_hbm.at[:, left], x.at[mine, :], scr.own.at[0]),
        pltpu.make_async_copy(g_hbm.at[:, left], g.at[mine, :], scr.own.at[1]),
    ]
    for copy in own:
        copy.start()
    bk[mine, :] = wk[...]
    ck[mine, :] = rk[...]
    raws[core] = raw[...]
    stage = scr.stage
    stage[...] = jnp.zeros_like(stage)
    stage[0:1, :few] = decay[...]
    stage[1:2, :few] = skip[...]
    stage[2:3, :few] = bias[...]
    scr.prm_got[me] = stage[...]
    pl.semaphore_wait(barrier, n + replicas - 2)

    def prm_copy(k):
        return send(stage, scr.prm_got.at[me], "prm", k, {"seq": seq(k)})

    key_copies = [
        send(src, dst, "key", j, {"seq": near})
        for j, (src, dst) in enumerate(((wk, bk.at[mine, :]), (rk, ck.at[mine, :]), (raw, raws.at[core])))
    ]

    def entry_copies(p):
        there = pl.ds(pl.multiple_of(near % 2 * span + p * LANES, LANES), LANES)
        here = pl.ds(pl.multiple_of(p * LANES, LANES), LANES)
        return [
            send(x_hbm.at[:, there], x.at[mine, here], "gox", p, {"seq": near}),
            send(g_hbm.at[:, there], g.at[mine, here], "gog", p, {"seq": near}),
        ]

    def state_copy(p):
        return send(scr.state.at[p], scr.state_got.at[p], "state", p, {"seq": far})

    def exit_copy(p):
        here = pl.ds(pl.multiple_of(p * LANES, LANES), LANES)
        there = pl.ds(pl.multiple_of(core * span + p * LANES, LANES), LANES)
        return send(dx.at[theirs, here], dx_out.at[:, there], "back", p, {"seq": near})

    for k in range(1, n):
        prm_copy(k).start()
    for copy in key_copies:
        copy.start()

    def launch(p, _):
        for copy in entry_copies(p):
            copy.start()
        return 0

    lax.fori_loop(0, pairs, launch, 0)
    for k in range(1, n):
        prm_copy(k).wait_recv()
    for copy in key_copies:
        copy.wait_recv()
    prm = scr.prm
    prm[...] = jnp.zeros_like(prm)
    prm[:, :few] = scr.prm_got[2 * core][:, :few]
    prm[:, few:heads] = scr.prm_got[2 * core + 1][:, :few]
    prepare(
        pick_heads(raws, core * heads, heads), prm[0:1, :heads], prm[2:3, :heads], scr.small,
        scr.arow, scr.acol, scr.dts, scr.sig, scr.rate, heads,
    )
    gains = jnp.broadcast_to(prm[1:2, :], (LANES, LANES)).T
    for h in range(heads):
        scr.skips[h] = jnp.broadcast_to(gains[h : h + 1, :], (8, LANES))
    a = jnp.concatenate([scr.arow[h, 0:1, :] for h in range(heads)], axis=0)
    tail = a[:, length - 1 :] - a + jnp.log(scr.dts[...]) * LOG2E
    reach = jnp.exp2(jnp.where(first, tail, a))
    reach = jnp.concatenate([reach, jnp.zeros((LANES - heads, length), f32)], axis=0).T
    for h in range(heads):
        scr.reach[h] = jnp.broadcast_to(reach[:, h : h + 1], (length, LANES))
    key = jnp.where(first, bk[...].astype(f32), ck[...].astype(f32))
    scr.key[...] = key.astype(bf16)
    scr.keyt[...] = key.T.astype(bf16)
    for copy in own:
        copy.wait()
    low = iota((length, LANES), 1) < LANES // 2
    low_row = iota((1, LANES), 1) < LANES // 2

    def weigh(p):
        here = pl.ds(pl.multiple_of(p * LANES, LANES), LANES)
        reach = jnp.where(low, scr.reach[2 * p], scr.reach[2 * p + 1])
        value = jnp.where(first, x[:, here].astype(f32), g[:, here].astype(f32))
        return here, reach, value

    def states(p, _):
        for copy in entry_copies(p):
            copy.wait_recv()
        _, reach, value = weigh(p)
        hi, lo = split_two(reach * value)
        kt = scr.keyt[...]
        scr.state[p] = dot_nn(kt, hi) + dot_nn(kt, lo)
        state_copy(p).start()
        return 0

    lax.fori_loop(0, pairs, states, 0)
    scores(bk, ck, scr, length)
    scr.col[...] = jnp.zeros_like(scr.col)

    def inside(p, _):
        gain = jnp.where(low_row, scr.skips[2 * p][0:1], scr.skips[2 * p + 1][0:1])
        one_pair(p, x, g, gain, dxf, scr, length)
        return 0

    lax.fori_loop(0, pairs, inside, 0)

    def write(i, db, dc):
        here = slice(i * LANES, (i + 1) * LANES)
        scr.dkeys[here, :LANES] = db
        scr.dkeys[here, LANES:] = dc

    key_grads(bk, ck, scr, length, write)
    scr.kcross[...] = jnp.zeros_like(scr.kcross)
    scr.zcross[...] = jnp.zeros_like(scr.zcross)
    lane = iota((length, LANES), 1)

    def across(p, _):
        state_copy(p).wait_recv()
        here, reach, value = weigh(p)
        shi, slo = split_two(scr.state_got[p])
        k = scr.key[...]
        u = reach * (dot_nn(k, shi) + dot_nn(k, slo))
        whi, wlo = split_two(reach * value)
        scr.kcross[...] += dot_nt(whi, shi) + (dot_nt(whi, slo) + dot_nt(wlo, shi))
        both = value * u
        one = jnp.sum(jnp.where(low, both, 0.0), axis=1, keepdims=True)
        two = jnp.sum(jnp.where(low, 0.0, both), axis=1, keepdims=True)
        scr.zcross[...] += jnp.where(lane == 2 * p, one, 0.0) + jnp.where(lane == 2 * p + 1, two, 0.0)
        dx[:, here] = (dxf[:, here] + jnp.where(first, u, 0.0)).astype(bf16)
        exit_copy(p).start()
        return 0

    lax.fori_loop(0, pairs, across, 0)
    keep = pltpu.make_async_copy(dx.at[mine, :], dx_out.at[:, left], scr.own.at[2])
    keep.start()
    kcross = scr.kcross[...]
    scr.dkeys[:, :LANES] += jnp.where(first, kcross, 0.0)
    scr.dkeys[:, LANES:] += jnp.where(first, 0.0, kcross)
    sum_copy = send(scr.dkeys.at[theirs, :], scr.dk_got, "dk", 0, {"seq": near})
    sum_copy.start()
    step_all, params = step_grads(scr, heads, length, (first, scr.zcross[...]))
    scr.par[...] = params

    def par_copy(k):
        return send(scr.par, scr.par_got.at[k], "par", k, {"dp": replica(k)})

    for k in range(1, replicas):
        par_copy(k).start()
    held = pl.ds(pl.multiple_of(core * heads, heads), heads)
    scr.step[...] = step_all.astype(bf16)
    step[held, :] = scr.step[:, mine]
    step_copy = send(scr.step.at[:, theirs], step.at[held, :], "st", 0, {"seq": near})
    step_copy.start()
    params = scr.par[...]
    for k in range(1, replicas):
        par_copy(k).wait_recv()
        params = params + scr.par_got[k]
    scr.tot[...] = params
    scr.tot_got[me] = params

    def tot_copy(k):
        return send(scr.tot, scr.tot_got.at[me], "tot", k, {"seq": seq(k)})

    for k in range(1, n):
        tot_copy(k).start()
    sum_copy.wait_recv()
    total = scr.dkeys[mine, :] + scr.dk_got[...]
    dwrite[...] = total[:, :LANES].astype(bf16)
    dread[...] = total[:, LANES:].astype(bf16)
    step_copy.wait_recv()
    for k in range(1, n):
        tot_copy(k).wait_recv()
    params = scr.tot_got[chip] + scr.tot_got[2 + chip]
    par[...] = jnp.where(core == 0, params[:3, :few], params[:3, few:heads]) / replicas
    keep.wait()

    def drain(p, _):
        for copy in entry_copies(p):
            copy.wait_send()
        state_copy(p).wait_send()
        exit_copy(p).wait()
        return 0

    lax.fori_loop(0, pairs, drain, 0)
    for copy in key_copies + [sum_copy, step_copy]:
        copy.wait_send()
    for k in range(1, n):
        prm_copy(k).wait_send()
        tot_copy(k).wait_send()
    for k in range(1, replicas):
        par_copy(k).wait_send()


def chip_backward(n, replicas, x, raw, wk, rk, g, decay, skip, bias):
    total, rows = raw.shape
    few = decay.shape[0]
    heads, length = 2 * few, 2 * rows
    pairs = heads // 2
    space = scratch(heads, length) | dict(
        x=pltpu.VMEM((length, pairs * LANES), bf16),
        g=pltpu.VMEM((length, pairs * LANES), bf16),
        dx=pltpu.VMEM((length, pairs * LANES), bf16),
        dxf=pltpu.VMEM((length, pairs * LANES), f32),
        bk=pltpu.VMEM((length, LANES), bf16),
        ck=pltpu.VMEM((length, LANES), bf16),
        key=pltpu.VMEM((length, LANES), bf16),
        keyt=pltpu.VMEM((LANES, length), bf16),
        raws=pltpu.VMEM((length // rows, total, rows), bf16),
        reach=pltpu.VMEM((heads, length, LANES), f32),
        skips=pltpu.VMEM((heads, 8, LANES), f32),
        state=pltpu.VMEM((pairs, LANES, LANES), f32),
        state_got=pltpu.VMEM((pairs, LANES, LANES), f32),
        kcross=pltpu.VMEM((length, LANES), f32),
        zcross=pltpu.VMEM((length, LANES), f32),
        dkeys=pltpu.VMEM((length, 2 * LANES), f32),
        dk_got=pltpu.VMEM((rows, 2 * LANES), f32),
        step=pltpu.VMEM((heads, length), bf16),
        stage=pltpu.VMEM((8, LANES), f32),
        prm=pltpu.VMEM((8, LANES), f32),
        prm_got=pltpu.VMEM((n, 8, LANES), f32),
        par=pltpu.VMEM((8, LANES), f32),
        par_got=pltpu.VMEM((replicas, 8, LANES), f32),
        tot=pltpu.VMEM((8, LANES), f32),
        tot_got=pltpu.VMEM((n, 8, LANES), f32),
        own=pltpu.SemaphoreType.DMA((3,)),
    )
    counts = dict(
        prm=n, key=3, gox=pairs, gog=pairs, state=pairs, back=pairs, dk=1, st=1, par=replicas, tot=n
    )
    for name, count in counts.items():
        space[name + "_out"] = pltpu.SemaphoreType.DMA((count,))
        space[name + "_in"] = pltpu.SemaphoreType.DMA((count,))
    vmem = pl.BlockSpec(memory_space=pltpu.VMEM)
    hbm = pl.BlockSpec(memory_space=pl.ANY)
    return pl.pallas_call(
        functools.partial(chip_kernel, tuple(space), n, replicas),
        out_shape=(
            jax.ShapeDtypeStruct(x.shape, bf16),
            jax.ShapeDtypeStruct(raw.shape, bf16),
            jax.ShapeDtypeStruct(wk.shape, bf16),
            jax.ShapeDtypeStruct(rk.shape, bf16),
            jax.ShapeDtypeStruct((3, few), f32),
        ),
        in_specs=[hbm, vmem, vmem, vmem, hbm, vmem, vmem, vmem],
        out_specs=(hbm, vmem, vmem, vmem, vmem),
        scratch_shapes=list(space.values()),
        compiler_params=pltpu.CompilerParams(
            vmem_limit_bytes=60 * 1024 * 1024, collective_id=1, has_side_effects=True
        ),
    )(x, raw, wk, rk, g, decay.reshape(1, few), skip.reshape(1, few), bias.reshape(1, few))


def settle(*refs):
    half = len(refs) // 2
    for src, dst in zip(refs[:half], refs[half:]):
        dst[...] = src[...]


def settled(arrays):
    steps = 4
    wide = arrays[0].shape[1] // steps
    blocks = [pl.BlockSpec((arrays[0].shape[0], wide), lambda i: (0, i))]
    blocks += [pl.BlockSpec(a.shape, lambda i: (0, 0)) for a in arrays[1:]]
    return pl.pallas_call(
        settle,
        grid=(steps,),
        out_shape=tuple(jax.ShapeDtypeStruct(a.shape, a.dtype) for a in arrays),
        in_specs=blocks,
        out_specs=tuple(blocks),
        compiler_params=pltpu.CompilerParams(vmem_limit_bytes=60 * 1024 * 1024),
    )(*arrays)


def shards(n, replicas, inputs, raw_step, write_keys, read_keys, grad_out, decay_log, skip_gain, step_bias):
    whole = chip_backward if n == 4 else backward
    dx, step, dwrite, dread, par = settled(whole(
        n, replicas, inputs[0], raw_step[0].T, write_keys[0], read_keys[0], grad_out[0],
        decay_log, skip_gain, step_bias,
    ))
    return dx[None], step.T[None], dwrite[None], dread[None], par


def solution(mesh):
    rows = P("dp", "seq", None)
    return jax.shard_map(
        functools.partial(shards, mesh.shape["seq"], mesh.shape["dp"]),
        mesh=mesh,
        in_specs=(rows,) * 5 + (P("seq"),) * 3,
        out_specs=(rows,) * 4 + (P(None, "seq"),),
        check_vma=False,
    )
```

```python
import functools
import types

import jax
import jax.numpy as jnp
from jax import lax
from jax.experimental import pallas as pl
from jax.experimental.pallas import tpu as pltpu
from jax.sharding import PartitionSpec as P

LANES = 128
ROWS = 16
LOG2E = 1.4426950408889634
bf16 = jnp.bfloat16
f32 = jnp.float32


def iota(shape, dim):
    return lax.broadcasted_iota(jnp.int32, shape, dim)


def dot_nt(a, b):
    return lax.dot_general(a, b, (((1,), (1,)), ((), ())), preferred_element_type=f32)


def dot_nn(a, b):
    return jnp.dot(a, b, preferred_element_type=f32)


def split_two(v):
    hi = v.astype(bf16)
    return hi, (v - hi.astype(f32)).astype(bf16)


def scan_lanes(v, reverse):
    rows, length = v.shape
    width = min(256, length)
    r, c = iota((width, width), 0), iota((width, width), 1)
    keep = (r >= c) if reverse else (r <= c)
    ones = jnp.where(keep, 1.0, 0.0).astype(bf16)
    one = v.astype(bf16)
    rest = v - one.astype(f32)
    two = rest.astype(bf16)
    three = (rest - two.astype(f32)).astype(bf16)
    stacked = jnp.concatenate([one, two, three], axis=0)
    spots = list(range(0, length, width))
    carry = jnp.zeros((rows, 1), f32)
    out = {}
    for start in reversed(spots) if reverse else spots:
        part = dot_nn(stacked[:, start : start + width], ones)
        part = part[:rows] + (part[rows : 2 * rows] + part[2 * rows :]) + carry
        out[start] = part
        carry = part[:, :1] if reverse else part[:, width - 1 :]
    return jnp.concatenate([out[s] for s in spots], axis=1)


def column(small, row, heads):
    small[0:1, :heads] = row
    return jnp.broadcast_to(small[0:1, :], (LANES, LANES)).T[:heads]


def pick_heads(raws, offset, heads):
    n, total, _ = raws.shape
    pick = jnp.where(iota((heads, total), 1) == iota((heads, total), 0) + offset, 1.0, 0.0)
    return jnp.concatenate([dot_nn(pick.astype(bf16), raws[k]) for k in range(n)], axis=1)


def prepare(z, decay, bias, small, arow, acol, dts, sig, rate, heads):
    length = z.shape[1]
    small[...] = jnp.zeros_like(small)
    z = z + column(small, bias, heads)[:, :1]
    rate_col = column(small, jnp.exp(decay), heads)
    rate[...] = rate_col
    dt = jnp.maximum(z, 0.0) + jnp.log1p(jnp.exp(-jnp.abs(z)))
    dts[...] = dt
    sig[...] = 1.0 / (1.0 + jnp.exp(-z))
    a = scan_lanes(dt * (rate_col[:, :1] * -LOG2E), False)
    for h in range(heads):
        arow[h] = jnp.broadcast_to(a[h : h + 1, :], (8, length))
    below = a - jnp.log(dt) * LOG2E
    down = jnp.concatenate([below, jnp.zeros((LANES - heads, length), f32)], axis=0).T
    for h in range(heads):
        acol[h] = jnp.broadcast_to(down[:, h : h + 1], (length, LANES))


def tile(pair, s0, t0, width, diagonal, x, g, scr):
    w, m, vacc = scr.w, scr.m, scr.vacc
    lanes = pl.ds(pl.multiple_of(pair * LANES, LANES), LANES)
    srows, trows = pl.ds(s0, LANES), pl.ds(t0, width)
    xs = x[srows, lanes]
    gs = g[trows, lanes]
    low = iota((width, LANES), 1) < LANES // 2
    zero = jnp.zeros_like(gs)
    parts = (jnp.where(low, gs, zero), jnp.where(low, zero, gs))
    for k in range(2):
        w[k, :, :width] = dot_nt(xs, parts[k])
    lane = iota((ROWS, LANES), 1)
    at = [scr.arow[2 * pair + k, :, trows] for k in range(2)]
    at = [jnp.concatenate([v] * (ROWS // 8), axis=0) for v in at]
    sums = [None, None]
    for c in range(LANES // ROWS):
        rows = pl.ds(s0 + c * ROWS, ROWS)
        here = slice(c * ROWS, (c + 1) * ROWS)
        s_tile = scr.score[rows, trows]
        q = scr.q[rows, trows]
        col = scr.col[rows, :]
        for k in range(2):
            ac = scr.acol[2 * pair + k, rows, :]
            gap = at[k] - jnp.concatenate([ac] * (width // LANES), axis=1)
            if diagonal:
                keep = iota((ROWS, width), 1) >= iota((ROWS, width), 0) + c * ROWS
                gap = jnp.where(keep, gap, -jnp.inf)
            lp = jnp.exp2(gap)
            wk = w[k, here, :width]
            q = q + lp * wk
            mk = lp * s_tile
            hi, lo = split_two(mk)
            m[2 * k, here, :width] = hi
            m[2 * k + 1, here, :width] = lo
            zk = mk * wk
            part = zk[:8] + zk[8:]
            sums[k] = part if sums[k] is None else sums[k] + part
            across = zk[:, :LANES]
            for j in range(1, width // LANES):
                across = across + zk[:, j * LANES : (j + 1) * LANES]
            total = jnp.sum(across, axis=1, keepdims=True)
            col = col + jnp.where(lane == 2 * pair + k, total, 0.0)
        scr.q[rows, trows] = q
        scr.col[rows, :] = col
    for k in range(2):
        scr.racc[k, :, trows] += sums[k]
    v = None
    for k in range(2):
        for j in range(2):
            term = dot_nn(m[2 * k + j, :, :width], parts[k])
            v = term if v is None else v + term
    return v


def one_pair(pair, x, g, gain, dx, scr, length):
    lanes = pl.ds(pl.multiple_of(pair * LANES, LANES), LANES)
    scr.racc[...] = jnp.zeros_like(scr.racc)
    low = iota((1, LANES), 1) < LANES // 2
    blocks = length // LANES

    def finish(s0, v):
        rows = pl.ds(s0, LANES)
        gs = g[rows, lanes].astype(f32)
        dx[rows, lanes] = (v + gain * gs).astype(dx.dtype)
        scr.direct[...] += jnp.sum(
            (x[rows, lanes].astype(f32) * gs).reshape(LANES // 8, 8, LANES), axis=0
        )

    scr.direct[...] = jnp.zeros_like(scr.direct)
    if blocks <= 4:
        for i in range(blocks):
            s0 = i * LANES
            finish(s0, tile(pair, s0, s0, length - s0, True, x, g, scr))
    else:

        def block(i, _):
            s0 = pl.multiple_of(i * LANES, LANES)
            scr.vacc[...] = tile(pair, s0, s0, LANES, True, x, g, scr)

            def right(j, _):
                t0 = pl.multiple_of(j * LANES, LANES)
                scr.vacc[...] += tile(pair, s0, t0, LANES, False, x, g, scr)
                return 0

            lax.fori_loop(i + 1, blocks, right, 0)
            finish(s0, scr.vacc[...])
            return 0

        lax.fori_loop(0, blocks, block, 0)
    direct = jnp.sum(scr.direct[...], axis=0, keepdims=True)
    for k in range(2):
        scr.row[pl.ds(2 * pair + k, 1), :] = jnp.sum(scr.racc[k], axis=0, keepdims=True)
        mine = jnp.where(low, direct, 0.0) if k == 0 else jnp.where(low, 0.0, direct)
        scr.gain[pl.ds(2 * pair + k, 1), :] = jnp.broadcast_to(
            jnp.sum(mine, axis=1, keepdims=True), (1, LANES)
        )


def scores(bk, ck, scr, length):
    blocks = length // LANES
    for i in range(blocks):
        s0 = i * LANES
        scr.score[s0 : s0 + LANES, s0:] = dot_nt(bk[s0 : s0 + LANES, :], ck[s0:, :])
        scr.q[s0 : s0 + LANES, s0:] = jnp.zeros((LANES, length - s0), f32)


def step_grads(scr, heads, length, cross=None):
    col = scr.col[...].T[:heads]
    row = scr.row[...]
    extra = 0.0
    if cross is not None:
        first, value = cross
        value = value.T[:heads]
        col = col + jnp.where(first, value, 0.0)
        row = row + jnp.where(first, 0.0, value)
        extra = jnp.where(first, jnp.sum(value, axis=1, keepdims=True), 0.0)
    dl = scan_lanes(row - col, True) + extra
    rate = scr.rate[:, :1]
    dt = scr.dts[...]
    ddt = col / dt - rate * dl
    draw = ddt * scr.sig[...]
    decay = -rate * jnp.sum(dl * dt, axis=1, keepdims=True)
    shift = jnp.sum(draw, axis=1, keepdims=True)
    lane = iota((heads, LANES), 1)
    params = jnp.where(lane == 0, decay, jnp.where(lane == 1, scr.gain[...], shift))
    params = jnp.concatenate([params, jnp.zeros((LANES - heads, LANES), f32)], axis=0).T
    return draw, params[:8]


def key_grads(bk, ck, scr, length, write):
    blocks = length // LANES
    bt = bk[...].astype(f32).T.astype(bf16)
    for i in range(blocks):
        here = slice(i * LANES, (i + 1) * LANES)
        hi, lo = split_two(scr.q[here, i * LANES :])
        db = dot_nn(hi, ck[i * LANES :, :]) + dot_nn(lo, ck[i * LANES :, :])
        upto = (i + 1) * LANES
        hi, lo = split_two(scr.q[:upto, here])
        dc = dot_nn(bt[:, :upto], hi) + dot_nn(bt[:, :upto], lo)
        write(i, db, dc.T)


def scratch(heads, length):
    width = length if length <= 4 * LANES else LANES
    return dict(
        small=pltpu.VMEM((8, LANES), f32),
        arow=pltpu.VMEM((heads, 8, length), f32),
        acol=pltpu.VMEM((heads, length, LANES), f32),
        dts=pltpu.VMEM((heads, length), f32),
        sig=pltpu.VMEM((heads, length), f32),
        rate=pltpu.VMEM((heads, LANES), f32),
        score=pltpu.VMEM((length, length), f32),
        q=pltpu.VMEM((length, length), f32),
        col=pltpu.VMEM((length, LANES), f32),
        row=pltpu.VMEM((heads, length), f32),
        gain=pltpu.VMEM((heads, LANES), f32),
        racc=pltpu.VMEM((2, 8, length), f32),
        direct=pltpu.VMEM((8, LANES), f32),
        vacc=pltpu.VMEM((LANES, LANES), f32),
        w=pltpu.VMEM((2, LANES, width), f32),
        m=pltpu.VMEM((4, LANES, width), bf16),
    )


def kernel(names, n, replicas, x_hbm, raw, wk, rk, g_hbm, decay, skip, bias, dx_out, step, dwrite, dread, par, *rest):
    scr = types.SimpleNamespace(**dict(zip(names, rest)))
    rows = x_hbm.shape[0]
    length = rows * n
    heads = decay.shape[1]
    pairs = heads // 2
    span = pairs * LANES
    me, dp = lax.axis_index("seq"), lax.axis_index("dp")
    x, g, dx, bk, ck, raws = (scr.x, scr.g, scr.dx, scr.bk, scr.ck, scr.raws)
    mine = pl.ds(pl.multiple_of(me * rows, rows), rows)
    left = pl.ds(pl.multiple_of(me * span, span), span)

    def seq(k):
        return lax.rem(me + k, n)

    def replica(k):
        return lax.rem(dp + k, replicas)

    def send(src, dst, out_sem, in_sem, target):
        return pltpu.make_async_remote_copy(
            src_ref=src, dst_ref=dst, send_sem=out_sem, recv_sem=in_sem,
            device_id=target, device_id_type=pl.DeviceIdType.MESH,
        )

    order = [k for k in range(1, n)]

    barrier = pltpu.get_barrier_semaphore()
    for k in range(1, n):
        pl.semaphore_signal(barrier, inc=1, device_id={"seq": seq(k)}, device_id_type=pl.DeviceIdType.MESH)
    for k in range(1, replicas):
        pl.semaphore_signal(barrier, inc=1, device_id={"dp": replica(k)}, device_id_type=pl.DeviceIdType.MESH)
    own = [
        pltpu.make_async_copy(x_hbm.at[:, left], x.at[mine, :], scr.own.at[0]),
        pltpu.make_async_copy(g_hbm.at[:, left], g.at[mine, :], scr.own.at[1]),
    ]
    for copy in own:
        copy.start()
    bk[mine, :] = wk[...]
    ck[mine, :] = rk[...]
    raws[me] = raw[...]
    pl.semaphore_wait(barrier, n + replicas - 2)

    def key_copies(k):
        target = {"seq": seq(k)}
        return [
            send(src, dst, scr.key_out.at[k, j], scr.key_in.at[k, j], target)
            for j, (src, dst) in enumerate(((wk, bk.at[mine, :]), (rk, ck.at[mine, :]), (raw, raws.at[me])))
        ]

    def entry_copies(p, k):
        target = seq(k)
        there = pl.ds(pl.multiple_of(target * span + p * LANES, LANES), LANES)
        here = pl.ds(pl.multiple_of(p * LANES, LANES), LANES)
        return [
            send(
                src.at[:, there], dst.at[mine, here], scr.go_out.at[p, k, j],
                scr.go_in.at[p, k, j], {"seq": target},
            )
            for j, (src, dst) in enumerate(((x_hbm, x), (g_hbm, g)))
        ]

    def exit_copy(p, k):
        target = seq(k)
        theirs = pl.ds(pl.multiple_of(target * rows, rows), rows)
        here = pl.ds(pl.multiple_of(p * LANES, LANES), LANES)
        there = pl.ds(pl.multiple_of(me * span + p * LANES, LANES), LANES)
        return send(
            dx.at[theirs, here], dx_out.at[:, there], scr.back_out.at[p, k],
            scr.back_in.at[p, k], {"seq": target},
        )

    for k in order:
        for copy in key_copies(k):
            copy.start()

    def launch(p, _):
        for k in order:
            for copy in entry_copies(p, k):
                copy.start()
        return 0

    lax.fori_loop(0, pairs, launch, 0)
    for k in order:
        for copy in key_copies(k):
            copy.wait_recv()
    prepare(
        pick_heads(raws, me * heads, heads), decay[...], bias[...], scr.small, scr.arow, scr.acol,
        scr.dts, scr.sig, scr.rate, heads,
    )
    scores(bk, ck, scr, length)
    scr.col[...] = jnp.zeros_like(scr.col)
    for copy in own:
        copy.wait()

    def body(p, _):
        for k in order:
            for copy in entry_copies(p, k):
                copy.wait_recv()
        low = iota((1, LANES), 1) < LANES // 2
        gain = jnp.where(low, skip[2 * p], skip[2 * p + 1])
        one_pair(p, x, g, gain, dx, scr, length)
        for k in order:
            exit_copy(p, k).start()
        return 0

    lax.fori_loop(0, pairs, body, 0)
    keep = pltpu.make_async_copy(dx.at[mine, :], dx_out.at[:, left], scr.own.at[2])
    keep.start()

    def write(i, db, dc):
        here = slice(i * LANES, (i + 1) * LANES)
        scr.dkeys[here, :LANES] = db
        scr.dkeys[here, LANES:] = dc

    key_grads(bk, ck, scr, length, write)

    def sum_copy(k):
        theirs = pl.ds(pl.multiple_of(seq(k) * rows, rows), rows)
        return send(
            scr.dkeys.at[theirs, :], scr.dk_got.at[k], scr.dk_out.at[k],
            scr.dk_in.at[k], {"seq": seq(k)},
        )

    for k in order:
        sum_copy(k).start()
    step_all, params = step_grads(scr, heads, length)
    spread = (raw.shape[0], heads)
    place = jnp.where(iota(spread, 1) + me * heads == iota(spread, 0), 1.0, 0.0)
    scr.step[...] = dot_nn(place.astype(bf16), step_all.astype(bf16)).astype(bf16)
    scr.par[...] = params

    def step_copy(k):
        theirs = pl.ds(pl.multiple_of(seq(k) * rows, rows), rows)
        return send(
            scr.step.at[:, theirs], scr.step_got.at[k], scr.st_out.at[k],
            scr.st_in.at[k], {"seq": seq(k)},
        )

    def par_copy(k):
        return send(
            scr.par, scr.par_got.at[k], scr.par_out.at[k], scr.par_in.at[k],
            {"dp": replica(k)},
        )

    for k in range(1, replicas):
        par_copy(k).start()
    for k in order:
        step_copy(k).start()

    total = scr.dkeys[mine, :]
    for k in order:
        sum_copy(k).wait_recv()
        total = total + scr.dk_got[k]
    dwrite[...] = total[:, :LANES].astype(bf16)
    dread[...] = total[:, LANES:].astype(bf16)
    steps = scr.step[:, mine].astype(f32)
    for k in order:
        step_copy(k).wait_recv()
        steps = steps + scr.step_got[k].astype(f32)
    step[...] = steps.astype(bf16)
    params = scr.par[...]
    for k in range(1, replicas):
        par_copy(k).wait_recv()
        params = params + scr.par_got[k]
    par[...] = params[:3, :heads] / replicas

    keep.wait()

    def drain(p, _):
        for k in order:
            for copy in entry_copies(p, k):
                copy.wait_send()
            exit_copy(p, k).wait()
        return 0

    lax.fori_loop(0, pairs, drain, 0)
    for k in order:
        for copy in key_copies(k):
            copy.wait_send()
        sum_copy(k).wait_send()
        step_copy(k).wait_send()
    for k in range(1, replicas):
        par_copy(k).wait_send()


def backward(n, replicas, x, raw, wk, rk, g, decay, skip, bias):
    total, rows = raw.shape
    heads, length = decay.shape[0], rows * n
    pairs = heads // 2
    dma = pltpu.SemaphoreType.DMA
    space = scratch(heads, length) | dict(
        x=pltpu.VMEM((length, pairs * LANES), bf16),
        g=pltpu.VMEM((length, pairs * LANES), bf16),
        dx=pltpu.VMEM((length, pairs * LANES), bf16),
        bk=pltpu.VMEM((length, LANES), bf16),
        ck=pltpu.VMEM((length, LANES), bf16),
        raws=pltpu.VMEM((length // rows, total, rows), bf16),
        dkeys=pltpu.VMEM((length, 2 * LANES), f32),
        dk_got=pltpu.VMEM((n, rows, 2 * LANES), f32),
        step=pltpu.VMEM((total, length), bf16),
        step_got=pltpu.VMEM((n, total, rows), bf16),
        par=pltpu.VMEM((8, LANES), f32),
        par_got=pltpu.VMEM((replicas, 8, LANES), f32),
        own=dma((3,)),
        key_out=dma((n, 3)),
        key_in=dma((n, 3)),
        go_out=dma((pairs, n, 2)),
        go_in=dma((pairs, n, 2)),
        back_out=dma((pairs, n)),
        back_in=dma((pairs, n)),
        dk_out=dma((n,)),
        dk_in=dma((n,)),
        st_out=dma((n,)),
        st_in=dma((n,)),
        par_out=dma((replicas,)),
        par_in=dma((replicas,)),
    )
    vmem = pl.BlockSpec(memory_space=pltpu.VMEM)
    smem = pl.BlockSpec(memory_space=pltpu.SMEM)
    hbm = pl.BlockSpec(memory_space=pl.ANY)
    return pl.pallas_call(
        functools.partial(kernel, tuple(space), n, replicas),
        out_shape=(
            jax.ShapeDtypeStruct(x.shape, bf16),
            jax.ShapeDtypeStruct(raw.shape, bf16),
            jax.ShapeDtypeStruct(wk.shape, bf16),
            jax.ShapeDtypeStruct(rk.shape, bf16),
            jax.ShapeDtypeStruct((3, heads), f32),
        ),
        in_specs=[hbm, vmem, vmem, vmem, hbm, vmem, smem, vmem],
        out_specs=(hbm, vmem, vmem, vmem, vmem),
        scratch_shapes=list(space.values()),
        compiler_params=pltpu.CompilerParams(
            vmem_limit_bytes=60 * 1024 * 1024, collective_id=0, has_side_effects=True
        ),
    )(x, raw, wk, rk, g, decay.reshape(1, heads), skip, bias.reshape(1, heads))


def chip_kernel(names, n, replicas, x_hbm, raw, wk, rk, g_hbm, decay, skip, bias, dx_out, step, dwrite, dread, par, *rest):
    scr = types.SimpleNamespace(**dict(zip(names, rest)))
    rows = x_hbm.shape[0]
    length = 2 * rows
    few = decay.shape[1]
    heads = 2 * few
    pairs = heads // 2
    span = pairs * LANES
    group = 4 if pairs % 4 == 0 else 1
    broad = group * LANES
    groups = pairs // group
    me, dp = lax.axis_index("seq"), lax.axis_index("dp")
    chip, core = me // 2, lax.rem(me, 2)
    first = chip == 0
    near, far = me + 1 - 2 * core, lax.rem(me + 2, n)
    x, g, bk, ck, raws = (scr.both.at[0], scr.both.at[1], scr.bk, scr.ck, scr.raws)
    dxf, dx = scr.dxf, scr.dx
    mine = pl.ds(pl.multiple_of(core * rows, rows), rows)
    theirs = pl.ds(pl.multiple_of((1 - core) * rows, rows), rows)
    left = pl.ds(pl.multiple_of(core * span, span), span)
    mesh_id = pl.DeviceIdType.MESH

    def seq(k):
        return lax.rem(me + k, n)

    def replica(k):
        return lax.rem(dp + k, replicas)

    def send(src, dst, name, at, target):
        return pltpu.make_async_remote_copy(
            src_ref=src, dst_ref=dst, send_sem=getattr(scr, name + "_out").at[at],
            recv_sem=getattr(scr, name + "_in").at[at], device_id=target, device_id_type=mesh_id,
        )

    barrier = pltpu.get_barrier_semaphore()
    for k in range(1, n):
        pl.semaphore_signal(barrier, inc=1, device_id={"seq": seq(k)}, device_id_type=mesh_id)
    for k in range(1, replicas):
        pl.semaphore_signal(barrier, inc=1, device_id={"dp": replica(k)}, device_id_type=mesh_id)
    own = [
        pltpu.make_async_copy(x_hbm.at[:, left], x.at[mine, :], scr.own.at[0]),
        pltpu.make_async_copy(g_hbm.at[:, left], g.at[mine, :], scr.own.at[1]),
    ]
    for copy in own:
        copy.start()
    bk[mine, :] = wk[...]
    ck[mine, :] = rk[...]
    raws[core] = raw[...]
    stage = scr.stage
    stage[...] = jnp.zeros_like(stage)
    stage[0:1, :few] = decay[...]
    stage[1:2, :few] = skip[...]
    stage[2:3, :few] = bias[...]
    scr.prm_got[me] = stage[...]
    pl.semaphore_wait(barrier, n + replicas - 2)

    def prm_copy(k):
        return send(stage, scr.prm_got.at[me], "prm", k, {"seq": seq(k)})

    key_copies = [
        send(src, dst, "key", j, {"seq": near})
        for j, (src, dst) in enumerate(((wk, bk.at[mine, :]), (rk, ck.at[mine, :]), (raw, raws.at[core])))
    ]

    def entry_copies(p):
        there = pl.ds(pl.multiple_of((1 - core) * span + p * broad, LANES), broad)
        here = pl.ds(pl.multiple_of(p * broad, LANES), broad)
        return [
            send(x_hbm.at[:, there], x.at[mine, here], "gox", p, {"seq": near}),
            send(g_hbm.at[:, there], g.at[mine, here], "gog", p, {"seq": near}),
        ]

    def state_copy(p):
        return send(scr.state.at[p], scr.state_got.at[p], "state", p, {"seq": far})

    def exit_copy(p):
        here = pl.ds(pl.multiple_of(p * broad, LANES), broad)
        there = pl.ds(pl.multiple_of(core * span + p * broad, LANES), broad)
        return send(dx.at[theirs, here], dx_out.at[:, there], "back", p, {"seq": near})

    for k in range(1, n):
        prm_copy(k).start()
    for copy in key_copies:
        copy.start()

    def launch(p, _):
        for copy in entry_copies(p):
            copy.start()
        return 0

    lax.fori_loop(0, groups, launch, 0)
    for k in range(1, n):
        prm_copy(k).wait_recv()
    for copy in key_copies:
        copy.wait_recv()
    prm = scr.prm
    prm[...] = jnp.zeros_like(prm)
    prm[:, :few] = scr.prm_got[2 * core][:, :few]
    prm[:, few:heads] = scr.prm_got[2 * core + 1][:, :few]
    prepare(
        pick_heads(raws, core * heads, heads), prm[0:1, :heads], prm[2:3, :heads], scr.small,
        scr.arow, scr.acol, scr.dts, scr.sig, scr.rate, heads,
    )
    gains = jnp.broadcast_to(prm[1:2, :], (LANES, LANES)).T
    for h in range(heads):
        scr.skips[h] = jnp.broadcast_to(gains[h : h + 1, :], (8, LANES))
    a = jnp.concatenate([scr.arow[h, 0:1, :] for h in range(heads)], axis=0)
    tail = a[:, length - 1 :] - a + jnp.log(scr.dts[...]) * LOG2E
    reach = jnp.exp2(jnp.where(first, tail, a))
    reach = jnp.concatenate([reach, jnp.zeros((LANES - heads, length), f32)], axis=0).T
    low = iota((length, LANES), 1) < LANES // 2
    for p in range(pairs):
        one, two = reach[:, 2 * p : 2 * p + 1], reach[:, 2 * p + 1 : 2 * p + 2]
        spot = p % group * LANES
        scr.reach[p // group, :, spot : spot + LANES] = jnp.where(low, one, two)
    key = jnp.where(first, bk[...].astype(f32), ck[...].astype(f32))
    scr.key[...] = key.astype(bf16)
    scr.keyt[...] = key.T.astype(bf16)
    for copy in own:
        copy.wait()
    low_row = iota((1, LANES), 1) < LANES // 2

    def states(q, _):
        for copy in entry_copies(q):
            copy.wait_recv()
        here = pl.ds(pl.multiple_of(q * broad, LANES), broad)
        hi, lo = split_two(scr.reach[q] * scr.both[chip, :, here].astype(f32))
        scr.high[q] = hi
        scr.rest[q] = lo
        kt = scr.keyt[...]
        scr.state[q] = dot_nn(kt, hi) + dot_nn(kt, lo)
        state_copy(q).start()
        return 0

    lax.fori_loop(0, groups, states, 0)
    scores(bk, ck, scr, length)
    scr.col[...] = jnp.zeros_like(scr.col)

    def inside(p, _):
        gain = jnp.where(low_row, scr.skips[2 * p][0:1], scr.skips[2 * p + 1][0:1])
        one_pair(p, x, g, gain, dxf, scr, length)
        return 0

    lax.fori_loop(0, pairs, inside, 0)

    def write(i, db, dc):
        here = slice(i * LANES, (i + 1) * LANES)
        scr.dkeys[here, :LANES] = db
        scr.dkeys[here, LANES:] = dc

    key_grads(bk, ck, scr, length, write)
    scr.kcross[...] = jnp.zeros_like(scr.kcross)
    scr.zcross[...] = jnp.zeros_like(scr.zcross)

    def across(q, _):
        state_copy(q).wait_recv()
        here = pl.ds(pl.multiple_of(q * broad, LANES), broad)
        shi, slo = split_two(scr.state_got[q])
        k = scr.key[...]
        whi, wlo = scr.high[q], scr.rest[q]
        u = scr.reach[q] * (dot_nn(k, shi) + dot_nn(k, slo))
        scr.kcross[...] += dot_nt(whi, shi) + (dot_nt(whi, slo) + dot_nt(wlo, shi))
        hi, lo = split_two(scr.both[chip, :, here].astype(f32) * u)
        head = 2 * group * q + iota((broad, LANES), 0) // (LANES // 2)
        pick = jnp.where(iota((broad, LANES), 1) == head, 1.0, 0.0).astype(bf16)
        scr.zcross[...] += dot_nn(hi, pick) + dot_nn(lo, pick)
        dx[:, here] = (dxf[:, here] + jnp.where(first, u, 0.0)).astype(bf16)
        exit_copy(q).start()
        return 0

    lax.fori_loop(0, groups, across, 0)
    keep = pltpu.make_async_copy(dx.at[mine, :], dx_out.at[:, left], scr.own.at[2])
    keep.start()
    kcross = scr.kcross[...]
    scr.dkeys[:, :LANES] += jnp.where(first, kcross, 0.0)
    scr.dkeys[:, LANES:] += jnp.where(first, 0.0, kcross)
    sum_copy = send(scr.dkeys.at[theirs, :], scr.dk_got, "dk", 0, {"seq": near})
    sum_copy.start()
    step_all, params = step_grads(scr, heads, length, (first, scr.zcross[...]))
    scr.par[...] = params

    def par_copy(k):
        return send(scr.par, scr.par_got.at[k], "par", k, {"dp": replica(k)})

    for k in range(1, replicas):
        par_copy(k).start()
    held = pl.ds(pl.multiple_of(core * heads, heads), heads)
    scr.step[...] = step_all.astype(bf16)
    step[held, :] = scr.step[:, mine]
    step_copy = send(scr.step.at[:, theirs], step.at[held, :], "st", 0, {"seq": near})
    step_copy.start()
    params = scr.par[...]
    for k in range(1, replicas):
        par_copy(k).wait_recv()
        params = params + scr.par_got[k]
    scr.tot[...] = params
    scr.tot_got[me] = params

    def tot_copy(k):
        return send(scr.tot, scr.tot_got.at[me], "tot", k, {"seq": seq(k)})

    for k in range(1, n):
        tot_copy(k).start()
    sum_copy.wait_recv()
    total = scr.dkeys[mine, :] + scr.dk_got[...]
    dwrite[...] = total[:, :LANES].astype(bf16)
    dread[...] = total[:, LANES:].astype(bf16)
    step_copy.wait_recv()
    for k in range(1, n):
        tot_copy(k).wait_recv()
    params = scr.tot_got[chip] + scr.tot_got[2 + chip]
    par[...] = jnp.where(core == 0, params[:3, :few], params[:3, few:heads]) / replicas
    keep.wait()

    def drain(p, _):
        for copy in entry_copies(p):
            copy.wait_send()
        state_copy(p).wait_send()
        exit_copy(p).wait()
        return 0

    lax.fori_loop(0, groups, drain, 0)
    for copy in key_copies + [sum_copy, step_copy]:
        copy.wait_send()
    for k in range(1, n):
        prm_copy(k).wait_send()
        tot_copy(k).wait_send()
    for k in range(1, replicas):
        par_copy(k).wait_send()


def chip_backward(n, replicas, x, raw, wk, rk, g, decay, skip, bias):
    total, rows = raw.shape
    few = decay.shape[0]
    heads, length = 2 * few, 2 * rows
    pairs = heads // 2
    group = 4 if pairs % 4 == 0 else 1
    groups, broad = pairs // group, group * LANES
    space = scratch(heads, length) | dict(
        both=pltpu.VMEM((2, length, pairs * LANES), bf16),
        high=pltpu.VMEM((groups, length, broad), bf16),
        rest=pltpu.VMEM((groups, length, broad), bf16),
        dx=pltpu.VMEM((length, pairs * LANES), bf16),
        dxf=pltpu.VMEM((length, pairs * LANES), f32),
        bk=pltpu.VMEM((length, LANES), bf16),
        ck=pltpu.VMEM((length, LANES), bf16),
        key=pltpu.VMEM((length, LANES), bf16),
        keyt=pltpu.VMEM((LANES, length), bf16),
        raws=pltpu.VMEM((length // rows, total, rows), bf16),
        reach=pltpu.VMEM((groups, length, broad), f32),
        skips=pltpu.VMEM((heads, 8, LANES), f32),
        state=pltpu.VMEM((groups, LANES, broad), f32),
        state_got=pltpu.VMEM((groups, LANES, broad), f32),
        kcross=pltpu.VMEM((length, LANES), f32),
        zcross=pltpu.VMEM((length, LANES), f32),
        dkeys=pltpu.VMEM((length, 2 * LANES), f32),
        dk_got=pltpu.VMEM((rows, 2 * LANES), f32),
        step=pltpu.VMEM((heads, length), bf16),
        stage=pltpu.VMEM((8, LANES), f32),
        prm=pltpu.VMEM((8, LANES), f32),
        prm_got=pltpu.VMEM((n, 8, LANES), f32),
        par=pltpu.VMEM((8, LANES), f32),
        par_got=pltpu.VMEM((replicas, 8, LANES), f32),
        tot=pltpu.VMEM((8, LANES), f32),
        tot_got=pltpu.VMEM((n, 8, LANES), f32),
        own=pltpu.SemaphoreType.DMA((3,)),
    )
    counts = dict(
        prm=n, key=3, gox=groups, gog=groups, state=groups, back=groups, dk=1, st=1, par=replicas, tot=n
    )
    for name, count in counts.items():
        space[name + "_out"] = pltpu.SemaphoreType.DMA((count,))
        space[name + "_in"] = pltpu.SemaphoreType.DMA((count,))
    vmem = pl.BlockSpec(memory_space=pltpu.VMEM)
    hbm = pl.BlockSpec(memory_space=pl.ANY)
    return pl.pallas_call(
        functools.partial(chip_kernel, tuple(space), n, replicas),
        out_shape=(
            jax.ShapeDtypeStruct(x.shape, bf16),
            jax.ShapeDtypeStruct(raw.shape, bf16),
            jax.ShapeDtypeStruct(wk.shape, bf16),
            jax.ShapeDtypeStruct(rk.shape, bf16),
            jax.ShapeDtypeStruct((3, few), f32),
        ),
        in_specs=[hbm, vmem, vmem, vmem, hbm, vmem, vmem, vmem],
        out_specs=(hbm, vmem, vmem, vmem, vmem),
        scratch_shapes=list(space.values()),
        compiler_params=pltpu.CompilerParams(
            vmem_limit_bytes=60 * 1024 * 1024, collective_id=1, has_side_effects=True
        ),
    )(x, raw, wk, rk, g, decay.reshape(1, few), skip.reshape(1, few), bias.reshape(1, few))


def settle(*refs):
    half = (len(refs) - 1) // 2
    sems = refs[-1]
    cuts = sems.shape[0]
    rows = refs[0].shape[0] // cuts
    copies = [
        pltpu.make_async_copy(
            refs[0].at[pl.ds(k * rows, rows), :], refs[half].at[pl.ds(k * rows, rows), :], sems.at[k]
        )
        for k in range(cuts)
    ]
    for copy in copies:
        copy.start()
    for src, dst in zip(refs[1:half], refs[half + 1 : -1]):
        dst[...] = src[...]
    for copy in copies:
        copy.wait()


def settled(arrays):
    hbm, vmem = pl.BlockSpec(memory_space=pl.ANY), pl.BlockSpec(memory_space=pltpu.VMEM)
    blocks = [hbm] + [vmem] * (len(arrays) - 1)
    return pl.pallas_call(
        settle,
        out_shape=tuple(jax.ShapeDtypeStruct(a.shape, a.dtype) for a in arrays),
        in_specs=blocks,
        out_specs=tuple(blocks),
        scratch_shapes=[pltpu.SemaphoreType.DMA((8,))],
        compiler_params=pltpu.CompilerParams(vmem_limit_bytes=60 * 1024 * 1024),
    )(*arrays)


def shards(n, replicas, inputs, raw_step, write_keys, read_keys, grad_out, decay_log, skip_gain, step_bias):
    whole = chip_backward if n == 4 else backward
    dx, step, dwrite, dread, par = settled(whole(
        n, replicas, inputs[0], raw_step[0].T, write_keys[0], read_keys[0], grad_out[0],
        decay_log, skip_gain, step_bias,
    ))
    return dx[None], step.T[None], dwrite[None], dread[None], par


def solution(mesh):
    rows = P("dp", "seq", None)
    return jax.shard_map(
        functools.partial(shards, mesh.shape["seq"], mesh.shape["dp"]),
        mesh=mesh,
        in_specs=(rows,) * 5 + (P("seq"),) * 3,
        out_specs=(rows,) * 4 + (P(None, "seq"),),
        check_vma=False,
    )
```

```python
import functools
import types

import jax
import jax.numpy as jnp
from jax import lax
from jax.experimental import pallas as pl
from jax.experimental.pallas import tpu as pltpu
from jax.sharding import PartitionSpec as P

LANES = 128
ROWS = 16
LOG2E = 1.4426950408889634
bf16 = jnp.bfloat16
f32 = jnp.float32


def iota(shape, dim):
    return lax.broadcasted_iota(jnp.int32, shape, dim)


def dot_nt(a, b):
    return lax.dot_general(a, b, (((1,), (1,)), ((), ())), preferred_element_type=f32)


def dot_nn(a, b):
    return jnp.dot(a, b, preferred_element_type=f32)


def split_two(v):
    hi = v.astype(bf16)
    return hi, (v - hi.astype(f32)).astype(bf16)


def scan_lanes(v, reverse):
    rows, length = v.shape
    width = min(256, length)
    r, c = iota((width, width), 0), iota((width, width), 1)
    keep = (r >= c) if reverse else (r <= c)
    ones = jnp.where(keep, 1.0, 0.0).astype(bf16)
    one = v.astype(bf16)
    rest = v - one.astype(f32)
    two = rest.astype(bf16)
    three = (rest - two.astype(f32)).astype(bf16)
    stacked = jnp.concatenate([one, two, three], axis=0)
    spots = list(range(0, length, width))
    carry = jnp.zeros((rows, 1), f32)
    out = {}
    for start in reversed(spots) if reverse else spots:
        part = dot_nn(stacked[:, start : start + width], ones)
        part = part[:rows] + (part[rows : 2 * rows] + part[2 * rows :]) + carry
        out[start] = part
        carry = part[:, :1] if reverse else part[:, width - 1 :]
    return jnp.concatenate([out[s] for s in spots], axis=1)


def column(small, row, heads):
    small[0:1, :heads] = row
    return jnp.broadcast_to(small[0:1, :], (LANES, LANES)).T[:heads]


def pick_heads(raws, offset, heads):
    n, total, _ = raws.shape
    pick = jnp.where(iota((heads, total), 1) == iota((heads, total), 0) + offset, 1.0, 0.0)
    return jnp.concatenate([dot_nn(pick.astype(bf16), raws[k]) for k in range(n)], axis=1)


def prepare(z, decay, bias, small, arow, acol, dts, sig, rate, heads):
    length = z.shape[1]
    small[...] = jnp.zeros_like(small)
    z = z + column(small, bias, heads)[:, :1]
    rate_col = column(small, jnp.exp(decay), heads)
    rate[...] = rate_col
    dt = jnp.maximum(z, 0.0) + jnp.log1p(jnp.exp(-jnp.abs(z)))
    dts[...] = dt
    sig[...] = 1.0 / (1.0 + jnp.exp(-z))
    a = scan_lanes(dt * (rate_col[:, :1] * -LOG2E), False)
    for h in range(heads):
        arow[h] = jnp.broadcast_to(a[h : h + 1, :], (8, length))
    below = a - jnp.log(dt) * LOG2E
    down = jnp.concatenate([below, jnp.zeros((LANES - heads, length), f32)], axis=0).T
    for h in range(heads):
        acol[h] = jnp.broadcast_to(down[:, h : h + 1], (length, LANES))


def tile(pair, s0, t0, width, diagonal, x, g, scr):
    w, m, vacc = scr.w, scr.m, scr.vacc
    lanes = pl.ds(pl.multiple_of(pair * LANES, LANES), LANES)
    srows, trows = pl.ds(s0, LANES), pl.ds(t0, width)
    xs = x[srows, lanes]
    gs = g[trows, lanes]
    low = iota((width, LANES), 1) < LANES // 2
    zero = jnp.zeros_like(gs)
    parts = (jnp.where(low, gs, zero), jnp.where(low, zero, gs))
    for k in range(2):
        w[k, :, :width] = dot_nt(xs, parts[k])
    lane = iota((ROWS, LANES), 1)
    at = [scr.arow[2 * pair + k, :, trows] for k in range(2)]
    at = [jnp.concatenate([v] * (ROWS // 8), axis=0) for v in at]
    sums = [None, None]
    for c in range(LANES // ROWS):
        rows = pl.ds(s0 + c * ROWS, ROWS)
        here = slice(c * ROWS, (c + 1) * ROWS)
        s_tile = scr.score[rows, trows]
        q = scr.q[rows, trows]
        col = scr.col[rows, :]
        for k in range(2):
            ac = scr.acol[2 * pair + k, rows, :]
            gap = at[k] - jnp.concatenate([ac] * (width // LANES), axis=1)
            if diagonal:
                keep = iota((ROWS, width), 1) >= iota((ROWS, width), 0) + c * ROWS
                gap = jnp.where(keep, gap, -jnp.inf)
            lp = jnp.exp2(gap)
            wk = w[k, here, :width]
            q = q + lp * wk
            mk = lp * s_tile
            hi, lo = split_two(mk)
            m[2 * k, here, :width] = hi
            m[2 * k + 1, here, :width] = lo
            zk = mk * wk
            part = zk[:8] + zk[8:]
            sums[k] = part if sums[k] is None else sums[k] + part
            across = zk[:, :LANES]
            for j in range(1, width // LANES):
                across = across + zk[:, j * LANES : (j + 1) * LANES]
            total = jnp.sum(across, axis=1, keepdims=True)
            col = col + jnp.where(lane == 2 * pair + k, total, 0.0)
        scr.q[rows, trows] = q
        scr.col[rows, :] = col
    for k in range(2):
        scr.racc[k, :, trows] += sums[k]
    v = None
    for k in range(2):
        for j in range(2):
            term = dot_nn(m[2 * k + j, :, :width], parts[k])
            v = term if v is None else v + term
    return v


def one_pair(pair, x, g, gain, dx, scr, length):
    lanes = pl.ds(pl.multiple_of(pair * LANES, LANES), LANES)
    scr.racc[...] = jnp.zeros_like(scr.racc)
    low = iota((1, LANES), 1) < LANES // 2
    blocks = length // LANES

    def finish(s0, v):
        rows = pl.ds(s0, LANES)
        gs = g[rows, lanes].astype(f32)
        dx[rows, lanes] = (v + gain * gs).astype(dx.dtype)
        scr.direct[...] += jnp.sum(
            (x[rows, lanes].astype(f32) * gs).reshape(LANES // 8, 8, LANES), axis=0
        )

    scr.direct[...] = jnp.zeros_like(scr.direct)
    if blocks <= 4:
        for i in range(blocks):
            s0 = i * LANES
            finish(s0, tile(pair, s0, s0, length - s0, True, x, g, scr))
    else:

        def block(i, _):
            s0 = pl.multiple_of(i * LANES, LANES)
            scr.vacc[...] = tile(pair, s0, s0, LANES, True, x, g, scr)

            def right(j, _):
                t0 = pl.multiple_of(j * LANES, LANES)
                scr.vacc[...] += tile(pair, s0, t0, LANES, False, x, g, scr)
                return 0

            lax.fori_loop(i + 1, blocks, right, 0)
            finish(s0, scr.vacc[...])
            return 0

        lax.fori_loop(0, blocks, block, 0)
    direct = jnp.sum(scr.direct[...], axis=0, keepdims=True)
    for k in range(2):
        scr.row[pl.ds(2 * pair + k, 1), :] = jnp.sum(scr.racc[k], axis=0, keepdims=True)
        mine = jnp.where(low, direct, 0.0) if k == 0 else jnp.where(low, 0.0, direct)
        scr.gain[pl.ds(2 * pair + k, 1), :] = jnp.broadcast_to(
            jnp.sum(mine, axis=1, keepdims=True), (1, LANES)
        )


def scores(bk, ck, scr, length):
    blocks = length // LANES
    for i in range(blocks):
        s0 = i * LANES
        scr.score[s0 : s0 + LANES, s0:] = dot_nt(bk[s0 : s0 + LANES, :], ck[s0:, :])
        scr.q[s0 : s0 + LANES, s0:] = jnp.zeros((LANES, length - s0), f32)


def step_grads(scr, heads, length, cross=None):
    col = scr.col[...].T[:heads]
    row = scr.row[...]
    extra = 0.0
    if cross is not None:
        first, value = cross
        value = value.T[:heads]
        col = col + jnp.where(first, value, 0.0)
        row = row + jnp.where(first, 0.0, value)
        extra = jnp.where(first, jnp.sum(value, axis=1, keepdims=True), 0.0)
    dl = scan_lanes(row - col, True) + extra
    rate = scr.rate[:, :1]
    dt = scr.dts[...]
    ddt = col / dt - rate * dl
    draw = ddt * scr.sig[...]
    decay = -rate * jnp.sum(dl * dt, axis=1, keepdims=True)
    shift = jnp.sum(draw, axis=1, keepdims=True)
    lane = iota((heads, LANES), 1)
    params = jnp.where(lane == 0, decay, jnp.where(lane == 1, scr.gain[...], shift))
    params = jnp.concatenate([params, jnp.zeros((LANES - heads, LANES), f32)], axis=0).T
    return draw, params[:8]


def key_grads(bk, ck, scr, length, write):
    blocks = length // LANES
    bt = bk[...].astype(f32).T.astype(bf16)
    for i in range(blocks):
        here = slice(i * LANES, (i + 1) * LANES)
        hi, lo = split_two(scr.q[here, i * LANES :])
        db = dot_nn(hi, ck[i * LANES :, :]) + dot_nn(lo, ck[i * LANES :, :])
        upto = (i + 1) * LANES
        hi, lo = split_two(scr.q[:upto, here])
        dc = dot_nn(bt[:, :upto], hi) + dot_nn(bt[:, :upto], lo)
        write(i, db, dc.T)


def scratch(heads, length):
    width = length if length <= 4 * LANES else LANES
    return dict(
        small=pltpu.VMEM((8, LANES), f32),
        arow=pltpu.VMEM((heads, 8, length), f32),
        acol=pltpu.VMEM((heads, length, LANES), f32),
        dts=pltpu.VMEM((heads, length), f32),
        sig=pltpu.VMEM((heads, length), f32),
        rate=pltpu.VMEM((heads, LANES), f32),
        score=pltpu.VMEM((length, length), f32),
        q=pltpu.VMEM((length, length), f32),
        col=pltpu.VMEM((length, LANES), f32),
        row=pltpu.VMEM((heads, length), f32),
        gain=pltpu.VMEM((heads, LANES), f32),
        racc=pltpu.VMEM((2, 8, length), f32),
        direct=pltpu.VMEM((8, LANES), f32),
        vacc=pltpu.VMEM((LANES, LANES), f32),
        w=pltpu.VMEM((2, LANES, width), f32),
        m=pltpu.VMEM((4, LANES, width), bf16),
    )


def kernel(names, n, replicas, x_hbm, raw, wk, rk, g_hbm, decay, skip, bias, dx_out, step, dwrite, dread, par, *rest):
    scr = types.SimpleNamespace(**dict(zip(names, rest)))
    rows = x_hbm.shape[0]
    length = rows * n
    heads = decay.shape[1]
    pairs = heads // 2
    span = pairs * LANES
    me, dp = lax.axis_index("seq"), lax.axis_index("dp")
    x, g, dx, bk, ck, raws = (scr.x, scr.g, scr.dx, scr.bk, scr.ck, scr.raws)
    mine = pl.ds(pl.multiple_of(me * rows, rows), rows)
    left = pl.ds(pl.multiple_of(me * span, span), span)

    def seq(k):
        return lax.rem(me + k, n)

    def replica(k):
        return lax.rem(dp + k, replicas)

    def send(src, dst, out_sem, in_sem, target):
        return pltpu.make_async_remote_copy(
            src_ref=src, dst_ref=dst, send_sem=out_sem, recv_sem=in_sem,
            device_id=target, device_id_type=pl.DeviceIdType.MESH,
        )

    order = [k for k in range(1, n)]

    barrier = pltpu.get_barrier_semaphore()
    for k in range(1, n):
        pl.semaphore_signal(barrier, inc=1, device_id={"seq": seq(k)}, device_id_type=pl.DeviceIdType.MESH)
    for k in range(1, replicas):
        pl.semaphore_signal(barrier, inc=1, device_id={"dp": replica(k)}, device_id_type=pl.DeviceIdType.MESH)
    own = [
        pltpu.make_async_copy(x_hbm.at[:, left], x.at[mine, :], scr.own.at[0]),
        pltpu.make_async_copy(g_hbm.at[:, left], g.at[mine, :], scr.own.at[1]),
    ]
    for copy in own:
        copy.start()
    bk[mine, :] = wk[...]
    ck[mine, :] = rk[...]
    raws[me] = raw[...]
    pl.semaphore_wait(barrier, n + replicas - 2)

    def key_copies(k):
        target = {"seq": seq(k)}
        return [
            send(src, dst, scr.key_out.at[k, j], scr.key_in.at[k, j], target)
            for j, (src, dst) in enumerate(((wk, bk.at[mine, :]), (rk, ck.at[mine, :]), (raw, raws.at[me])))
        ]

    def entry_copies(p, k):
        target = seq(k)
        there = pl.ds(pl.multiple_of(target * span + p * LANES, LANES), LANES)
        here = pl.ds(pl.multiple_of(p * LANES, LANES), LANES)
        return [
            send(
                src.at[:, there], dst.at[mine, here], scr.go_out.at[p, k, j],
                scr.go_in.at[p, k, j], {"seq": target},
            )
            for j, (src, dst) in enumerate(((x_hbm, x), (g_hbm, g)))
        ]

    def exit_copy(p, k):
        target = seq(k)
        theirs = pl.ds(pl.multiple_of(target * rows, rows), rows)
        here = pl.ds(pl.multiple_of(p * LANES, LANES), LANES)
        there = pl.ds(pl.multiple_of(me * span + p * LANES, LANES), LANES)
        return send(
            dx.at[theirs, here], dx_out.at[:, there], scr.back_out.at[p, k],
            scr.back_in.at[p, k], {"seq": target},
        )

    for k in order:
        for copy in key_copies(k):
            copy.start()

    def launch(p, _):
        for k in order:
            for copy in entry_copies(p, k):
                copy.start()
        return 0

    lax.fori_loop(0, pairs, launch, 0)
    for k in order:
        for copy in key_copies(k):
            copy.wait_recv()
    prepare(
        pick_heads(raws, me * heads, heads), decay[...], bias[...], scr.small, scr.arow, scr.acol,
        scr.dts, scr.sig, scr.rate, heads,
    )
    scores(bk, ck, scr, length)
    scr.col[...] = jnp.zeros_like(scr.col)
    for copy in own:
        copy.wait()

    def body(p, _):
        for k in order:
            for copy in entry_copies(p, k):
                copy.wait_recv()
        low = iota((1, LANES), 1) < LANES // 2
        gain = jnp.where(low, skip[2 * p], skip[2 * p + 1])
        one_pair(p, x, g, gain, dx, scr, length)
        for k in order:
            exit_copy(p, k).start()
        return 0

    lax.fori_loop(0, pairs, body, 0)
    keep = pltpu.make_async_copy(dx.at[mine, :], dx_out.at[:, left], scr.own.at[2])
    keep.start()

    def write(i, db, dc):
        here = slice(i * LANES, (i + 1) * LANES)
        scr.dkeys[here, :LANES] = db
        scr.dkeys[here, LANES:] = dc

    key_grads(bk, ck, scr, length, write)

    def sum_copy(k):
        theirs = pl.ds(pl.multiple_of(seq(k) * rows, rows), rows)
        return send(
            scr.dkeys.at[theirs, :], scr.dk_got.at[k], scr.dk_out.at[k],
            scr.dk_in.at[k], {"seq": seq(k)},
        )

    for k in order:
        sum_copy(k).start()
    step_all, params = step_grads(scr, heads, length)
    spread = (raw.shape[0], heads)
    place = jnp.where(iota(spread, 1) + me * heads == iota(spread, 0), 1.0, 0.0)
    scr.step[...] = dot_nn(place.astype(bf16), step_all.astype(bf16)).astype(bf16)
    scr.par[...] = params

    def step_copy(k):
        theirs = pl.ds(pl.multiple_of(seq(k) * rows, rows), rows)
        return send(
            scr.step.at[:, theirs], scr.step_got.at[k], scr.st_out.at[k],
            scr.st_in.at[k], {"seq": seq(k)},
        )

    def par_copy(k):
        return send(
            scr.par, scr.par_got.at[k], scr.par_out.at[k], scr.par_in.at[k],
            {"dp": replica(k)},
        )

    for k in range(1, replicas):
        par_copy(k).start()
    for k in order:
        step_copy(k).start()

    total = scr.dkeys[mine, :]
    for k in order:
        sum_copy(k).wait_recv()
        total = total + scr.dk_got[k]
    dwrite[...] = total[:, :LANES].astype(bf16)
    dread[...] = total[:, LANES:].astype(bf16)
    steps = scr.step[:, mine].astype(f32)
    for k in order:
        step_copy(k).wait_recv()
        steps = steps + scr.step_got[k].astype(f32)
    step[...] = steps.astype(bf16)
    params = scr.par[...]
    for k in range(1, replicas):
        par_copy(k).wait_recv()
        params = params + scr.par_got[k]
    par[...] = params[:3, :heads] / replicas

    keep.wait()

    def drain(p, _):
        for k in order:
            for copy in entry_copies(p, k):
                copy.wait_send()
            exit_copy(p, k).wait()
        return 0

    lax.fori_loop(0, pairs, drain, 0)
    for k in order:
        for copy in key_copies(k):
            copy.wait_send()
        sum_copy(k).wait_send()
        step_copy(k).wait_send()
    for k in range(1, replicas):
        par_copy(k).wait_send()


def backward(n, replicas, x, raw, wk, rk, g, decay, skip, bias):
    total, rows = raw.shape
    heads, length = decay.shape[0], rows * n
    pairs = heads // 2
    dma = pltpu.SemaphoreType.DMA
    space = scratch(heads, length) | dict(
        x=pltpu.VMEM((length, pairs * LANES), bf16),
        g=pltpu.VMEM((length, pairs * LANES), bf16),
        dx=pltpu.VMEM((length, pairs * LANES), bf16),
        bk=pltpu.VMEM((length, LANES), bf16),
        ck=pltpu.VMEM((length, LANES), bf16),
        raws=pltpu.VMEM((length // rows, total, rows), bf16),
        dkeys=pltpu.VMEM((length, 2 * LANES), f32),
        dk_got=pltpu.VMEM((n, rows, 2 * LANES), f32),
        step=pltpu.VMEM((total, length), bf16),
        step_got=pltpu.VMEM((n, total, rows), bf16),
        par=pltpu.VMEM((8, LANES), f32),
        par_got=pltpu.VMEM((replicas, 8, LANES), f32),
        own=dma((3,)),
        key_out=dma((n, 3)),
        key_in=dma((n, 3)),
        go_out=dma((pairs, n, 2)),
        go_in=dma((pairs, n, 2)),
        back_out=dma((pairs, n)),
        back_in=dma((pairs, n)),
        dk_out=dma((n,)),
        dk_in=dma((n,)),
        st_out=dma((n,)),
        st_in=dma((n,)),
        par_out=dma((replicas,)),
        par_in=dma((replicas,)),
    )
    vmem = pl.BlockSpec(memory_space=pltpu.VMEM)
    smem = pl.BlockSpec(memory_space=pltpu.SMEM)
    hbm = pl.BlockSpec(memory_space=pl.ANY)
    return pl.pallas_call(
        functools.partial(kernel, tuple(space), n, replicas),
        out_shape=(
            jax.ShapeDtypeStruct(x.shape, bf16),
            jax.ShapeDtypeStruct(raw.shape, bf16),
            jax.ShapeDtypeStruct(wk.shape, bf16),
            jax.ShapeDtypeStruct(rk.shape, bf16),
            jax.ShapeDtypeStruct((3, heads), f32),
        ),
        in_specs=[hbm, vmem, vmem, vmem, hbm, vmem, smem, vmem],
        out_specs=(hbm, vmem, vmem, vmem, vmem),
        scratch_shapes=list(space.values()),
        compiler_params=pltpu.CompilerParams(
            vmem_limit_bytes=60 * 1024 * 1024, collective_id=0, has_side_effects=True
        ),
    )(x, raw, wk, rk, g, decay.reshape(1, heads), skip, bias.reshape(1, heads))


def chip_kernel(names, n, replicas, x_hbm, raw, wk, rk, g_hbm, decay, skip, bias, dx_out, step, dwrite, dread, par, *rest):
    scr = types.SimpleNamespace(**dict(zip(names, rest)))
    rows = x_hbm.shape[0]
    length = 2 * rows
    few = decay.shape[1]
    heads = 2 * few
    pairs = heads // 2
    span = pairs * LANES
    group = 4 if pairs % 4 == 0 else 1
    broad = group * LANES
    groups = pairs // group
    me, dp = lax.axis_index("seq"), lax.axis_index("dp")
    chip, core = me // 2, lax.rem(me, 2)
    first = chip == 0
    near, far = me + 1 - 2 * core, lax.rem(me + 2, n)
    x, g, bk, ck, raws = (scr.both.at[0], scr.both.at[1], scr.bk, scr.ck, scr.raws)
    dxf, dx = scr.dxf, scr.dx
    mine = pl.ds(pl.multiple_of(core * rows, rows), rows)
    theirs = pl.ds(pl.multiple_of((1 - core) * rows, rows), rows)
    left = pl.ds(pl.multiple_of(core * span, span), span)
    mesh_id = pl.DeviceIdType.MESH

    def seq(k):
        return lax.rem(me + k, n)

    def replica(k):
        return lax.rem(dp + k, replicas)

    def send(src, dst, name, at, target):
        return pltpu.make_async_remote_copy(
            src_ref=src, dst_ref=dst, send_sem=getattr(scr, name + "_out").at[at],
            recv_sem=getattr(scr, name + "_in").at[at], device_id=target, device_id_type=mesh_id,
        )

    barrier = pltpu.get_barrier_semaphore()
    for k in range(1, n):
        pl.semaphore_signal(barrier, inc=1, device_id={"seq": seq(k)}, device_id_type=mesh_id)
    for k in range(1, replicas):
        pl.semaphore_signal(barrier, inc=1, device_id={"dp": replica(k)}, device_id_type=mesh_id)
    own = [
        pltpu.make_async_copy(x_hbm.at[:, left], x.at[mine, :], scr.own.at[0]),
        pltpu.make_async_copy(g_hbm.at[:, left], g.at[mine, :], scr.own.at[1]),
    ]
    for copy in own:
        copy.start()
    bk[mine, :] = wk[...]
    ck[mine, :] = rk[...]
    raws[core] = raw[...]
    stage = scr.stage
    stage[...] = jnp.zeros_like(stage)
    stage[0:1, :few] = decay[...]
    stage[1:2, :few] = skip[...]
    stage[2:3, :few] = bias[...]
    scr.prm_got[me] = stage[...]
    pl.semaphore_wait(barrier, n + replicas - 2)

    def prm_copy(k):
        return send(stage, scr.prm_got.at[me], "prm", k, {"seq": seq(k)})

    key_copies = [
        send(src, dst, "key", j, {"seq": near})
        for j, (src, dst) in enumerate(((wk, bk.at[mine, :]), (rk, ck.at[mine, :]), (raw, raws.at[core])))
    ]

    def entry_copies(p):
        there = pl.ds(pl.multiple_of((1 - core) * span + p * broad, LANES), broad)
        here = pl.ds(pl.multiple_of(p * broad, LANES), broad)
        return [
            send(x_hbm.at[:, there], x.at[mine, here], "gox", p, {"seq": near}),
            send(g_hbm.at[:, there], g.at[mine, here], "gog", p, {"seq": near}),
        ]

    def state_copy(p):
        return send(scr.state.at[p], scr.state_got.at[p], "state", p, {"seq": far})

    def exit_copy(p):
        here = pl.ds(pl.multiple_of(p * broad, LANES), broad)
        there = pl.ds(pl.multiple_of(core * span + p * broad, LANES), broad)
        return send(dx.at[theirs, here], dx_out.at[:, there], "back", p, {"seq": near})

    for k in range(1, n):
        prm_copy(k).start()
    for copy in key_copies:
        copy.start()

    def launch(p, _):
        for copy in entry_copies(p):
            copy.start()
        return 0

    lax.fori_loop(0, groups, launch, 0)
    for k in range(1, n):
        prm_copy(k).wait_recv()
    for copy in key_copies:
        copy.wait_recv()
    prm = scr.prm
    prm[...] = jnp.zeros_like(prm)
    prm[:, :few] = scr.prm_got[2 * core][:, :few]
    prm[:, few:heads] = scr.prm_got[2 * core + 1][:, :few]
    prepare(
        pick_heads(raws, core * heads, heads), prm[0:1, :heads], prm[2:3, :heads], scr.small,
        scr.arow, scr.acol, scr.dts, scr.sig, scr.rate, heads,
    )
    gains = jnp.broadcast_to(prm[1:2, :], (LANES, LANES)).T
    for h in range(heads):
        scr.skips[h] = jnp.broadcast_to(gains[h : h + 1, :], (8, LANES))
    a = jnp.concatenate([scr.arow[h, 0:1, :] for h in range(heads)], axis=0)
    tail = a[:, length - 1 :] - a + jnp.log(scr.dts[...]) * LOG2E
    reach = jnp.exp2(jnp.where(first, tail, a))
    reach = jnp.concatenate([reach, jnp.zeros((LANES - heads, length), f32)], axis=0).T
    low = iota((length, LANES), 1) < LANES // 2
    for p in range(pairs):
        one, two = reach[:, 2 * p : 2 * p + 1], reach[:, 2 * p + 1 : 2 * p + 2]
        spot = p % group * LANES
        scr.reach[p // group, :, spot : spot + LANES] = jnp.where(low, one, two)
    key = jnp.where(first, bk[...].astype(f32), ck[...].astype(f32))
    scr.key[...] = key.astype(bf16)
    scr.keyt[...] = key.T.astype(bf16)
    for copy in own:
        copy.wait()
    low_row = iota((1, LANES), 1) < LANES // 2

    def states(q, _):
        for copy in entry_copies(q):
            copy.wait_recv()
        here = pl.ds(pl.multiple_of(q * broad, LANES), broad)
        hi, lo = split_two(scr.reach[q] * scr.both[chip, :, here].astype(f32))
        scr.high[q] = hi
        scr.rest[q] = lo
        kt = scr.keyt[...]
        scr.state[q] = dot_nn(kt, hi) + dot_nn(kt, lo)
        state_copy(q).start()
        return 0

    lax.fori_loop(0, groups, states, 0)
    scores(bk, ck, scr, length)
    scr.col[...] = jnp.zeros_like(scr.col)

    def inside(p, _):
        gain = jnp.where(low_row, scr.skips[2 * p][0:1], scr.skips[2 * p + 1][0:1])
        one_pair(p, x, g, gain, dxf, scr, length)
        return 0

    lax.fori_loop(0, pairs, inside, 0)

    def write(i, db, dc):
        here = slice(i * LANES, (i + 1) * LANES)
        scr.dkeys[here, :LANES] = db
        scr.dkeys[here, LANES:] = dc

    key_grads(bk, ck, scr, length, write)
    scr.kcross[...] = jnp.zeros_like(scr.kcross)
    scr.zcross[...] = jnp.zeros_like(scr.zcross)

    def across(q, _):
        state_copy(q).wait_recv()
        here = pl.ds(pl.multiple_of(q * broad, LANES), broad)
        shi, slo = split_two(scr.state_got[q])
        k = scr.key[...]
        whi, wlo = scr.high[q], scr.rest[q]
        u = scr.reach[q] * (dot_nn(k, shi) + dot_nn(k, slo))
        scr.kcross[...] += dot_nt(whi, shi) + (dot_nt(whi, slo) + dot_nt(wlo, shi))
        hi, lo = split_two(scr.both[chip, :, here].astype(f32) * u)
        head = 2 * group * q + iota((broad, LANES), 0) // (LANES // 2)
        pick = jnp.where(iota((broad, LANES), 1) == head, 1.0, 0.0).astype(bf16)
        scr.zcross[...] += dot_nn(hi, pick) + dot_nn(lo, pick)
        dx[:, here] = (dxf[:, here] + jnp.where(first, u, 0.0)).astype(bf16)
        exit_copy(q).start()
        return 0

    lax.fori_loop(0, groups, across, 0)
    keep = pltpu.make_async_copy(dx.at[mine, :], dx_out.at[:, left], scr.own.at[2])
    keep.start()
    kcross = scr.kcross[...]
    scr.dkeys[:, :LANES] += jnp.where(first, kcross, 0.0)
    scr.dkeys[:, LANES:] += jnp.where(first, 0.0, kcross)
    sum_copy = send(scr.dkeys.at[theirs, :], scr.dk_got, "dk", 0, {"seq": near})
    sum_copy.start()
    step_all, params = step_grads(scr, heads, length, (first, scr.zcross[...]))
    scr.par[...] = params

    def par_copy(k):
        return send(scr.par, scr.par_got.at[k], "par", k, {"dp": replica(k)})

    for k in range(1, replicas):
        par_copy(k).start()
    held = pl.ds(pl.multiple_of(core * heads, heads), heads)
    scr.step[...] = step_all.astype(bf16)
    step[held, :] = scr.step[:, mine]
    step_copy = send(scr.step.at[:, theirs], step.at[held, :], "st", 0, {"seq": near})
    step_copy.start()
    params = scr.par[...]
    for k in range(1, replicas):
        par_copy(k).wait_recv()
        params = params + scr.par_got[k]
    scr.tot[...] = params
    scr.tot_got[me] = params

    def tot_copy(k):
        return send(scr.tot, scr.tot_got.at[me], "tot", k, {"seq": seq(k)})

    for k in range(1, n):
        tot_copy(k).start()
    sum_copy.wait_recv()
    total = scr.dkeys[mine, :] + scr.dk_got[...]
    dwrite[...] = total[:, :LANES].astype(bf16)
    dread[...] = total[:, LANES:].astype(bf16)
    step_copy.wait_recv()
    for k in range(1, n):
        tot_copy(k).wait_recv()
    params = scr.tot_got[chip] + scr.tot_got[2 + chip]
    par[...] = jnp.where(core == 0, params[:3, :few], params[:3, few:heads]) / replicas
    keep.wait()

    def drain(p, _):
        for copy in entry_copies(p):
            copy.wait_send()
        state_copy(p).wait_send()
        exit_copy(p).wait()
        return 0

    lax.fori_loop(0, groups, drain, 0)
    for copy in key_copies + [sum_copy, step_copy]:
        copy.wait_send()
    for k in range(1, n):
        prm_copy(k).wait_send()
        tot_copy(k).wait_send()
    for k in range(1, replicas):
        par_copy(k).wait_send()


def chip_backward(n, replicas, x, raw, wk, rk, g, decay, skip, bias):
    total, rows = raw.shape
    few = decay.shape[0]
    heads, length = 2 * few, 2 * rows
    pairs = heads // 2
    group = 4 if pairs % 4 == 0 else 1
    groups, broad = pairs // group, group * LANES
    space = scratch(heads, length) | dict(
        both=pltpu.VMEM((2, length, pairs * LANES), bf16),
        high=pltpu.VMEM((groups, length, broad), bf16),
        rest=pltpu.VMEM((groups, length, broad), bf16),
        dx=pltpu.VMEM((length, pairs * LANES), bf16),
        dxf=pltpu.VMEM((length, pairs * LANES), f32),
        bk=pltpu.VMEM((length, LANES), bf16),
        ck=pltpu.VMEM((length, LANES), bf16),
        key=pltpu.VMEM((length, LANES), bf16),
        keyt=pltpu.VMEM((LANES, length), bf16),
        raws=pltpu.VMEM((length // rows, total, rows), bf16),
        reach=pltpu.VMEM((groups, length, broad), f32),
        skips=pltpu.VMEM((heads, 8, LANES), f32),
        state=pltpu.VMEM((groups, LANES, broad), f32),
        state_got=pltpu.VMEM((groups, LANES, broad), f32),
        kcross=pltpu.VMEM((length, LANES), f32),
        zcross=pltpu.VMEM((length, LANES), f32),
        dkeys=pltpu.VMEM((length, 2 * LANES), f32),
        dk_got=pltpu.VMEM((rows, 2 * LANES), f32),
        step=pltpu.VMEM((heads, length), bf16),
        stage=pltpu.VMEM((8, LANES), f32),
        prm=pltpu.VMEM((8, LANES), f32),
        prm_got=pltpu.VMEM((n, 8, LANES), f32),
        par=pltpu.VMEM((8, LANES), f32),
        par_got=pltpu.VMEM((replicas, 8, LANES), f32),
        tot=pltpu.VMEM((8, LANES), f32),
        tot_got=pltpu.VMEM((n, 8, LANES), f32),
        own=pltpu.SemaphoreType.DMA((3,)),
    )
    counts = dict(
        prm=n, key=3, gox=groups, gog=groups, state=groups, back=groups, dk=1, st=1, par=replicas, tot=n
    )
    for name, count in counts.items():
        space[name + "_out"] = pltpu.SemaphoreType.DMA((count,))
        space[name + "_in"] = pltpu.SemaphoreType.DMA((count,))
    vmem = pl.BlockSpec(memory_space=pltpu.VMEM)
    hbm = pl.BlockSpec(memory_space=pl.ANY)
    return pl.pallas_call(
        functools.partial(chip_kernel, tuple(space), n, replicas),
        out_shape=(
            jax.ShapeDtypeStruct(x.shape, bf16),
            jax.ShapeDtypeStruct(raw.shape, bf16),
            jax.ShapeDtypeStruct(wk.shape, bf16),
            jax.ShapeDtypeStruct(rk.shape, bf16),
            jax.ShapeDtypeStruct((3, few), f32),
        ),
        in_specs=[hbm, vmem, vmem, vmem, hbm, vmem, vmem, vmem],
        out_specs=(hbm, vmem, vmem, vmem, vmem),
        scratch_shapes=list(space.values()),
        compiler_params=pltpu.CompilerParams(
            vmem_limit_bytes=60 * 1024 * 1024, collective_id=1, has_side_effects=True
        ),
    )(x, raw, wk, rk, g, decay.reshape(1, few), skip.reshape(1, few), bias.reshape(1, few))


def settle(*refs):
    half = (len(refs) - 3) // 2
    held, arrive, leave = refs[-3:]
    cuts = arrive.shape[0]
    rows = refs[0].shape[0] // cuts
    spots = [pl.ds(k * rows, rows) for k in range(cuts)]
    ins = [pltpu.make_async_copy(refs[0].at[s, :], held.at[s, :], arrive.at[k]) for k, s in enumerate(spots)]
    outs = [pltpu.make_async_copy(held.at[s, :], refs[half].at[s, :], leave.at[k]) for k, s in enumerate(spots)]
    for copy in ins:
        copy.start()
    for src, dst in zip(refs[1:half], refs[half + 1 : -3]):
        dst[...] = src[...]
    for one, two in zip(ins, outs):
        one.wait()
        two.start()
    for copy in outs:
        copy.wait()


def settled(arrays):
    hbm, vmem = pl.BlockSpec(memory_space=pl.ANY), pl.BlockSpec(memory_space=pltpu.VMEM)
    blocks = [hbm] + [vmem] * (len(arrays) - 1)
    return pl.pallas_call(
        settle,
        out_shape=tuple(jax.ShapeDtypeStruct(a.shape, a.dtype) for a in arrays),
        in_specs=blocks,
        out_specs=tuple(blocks),
        scratch_shapes=[
            pltpu.VMEM(arrays[0].shape, bf16),
            pltpu.SemaphoreType.DMA((4,)),
            pltpu.SemaphoreType.DMA((4,)),
        ],
        compiler_params=pltpu.CompilerParams(vmem_limit_bytes=60 * 1024 * 1024),
    )(*arrays)


def shards(n, replicas, inputs, raw_step, write_keys, read_keys, grad_out, decay_log, skip_gain, step_bias):
    whole = chip_backward if n == 4 else backward
    dx, step, dwrite, dread, par = settled(whole(
        n, replicas, inputs[0], raw_step[0].T, write_keys[0], read_keys[0], grad_out[0],
        decay_log, skip_gain, step_bias,
    ))
    return dx[None], step.T[None], dwrite[None], dread[None], par


def solution(mesh):
    rows = P("dp", "seq", None)
    return jax.shard_map(
        functools.partial(shards, mesh.shape["seq"], mesh.shape["dp"]),
        mesh=mesh,
        in_specs=(rows,) * 5 + (P("seq"),) * 3,
        out_specs=(rows,) * 4 + (P(None, "seq"),),
        check_vma=False,
    )
```
